128 devices in a mesh: src: 8 (over z, core), tgt: 16 (over y, x).
Axes of the slice: x: 4, y: 4, z: 4, core: 2. Of those that a mesh axis runs over, the one named last changes fastest.
Arguments:
- src_points: bfloat16 [16384, 512], P(('src', 'tgt')), may hold values from -1 to 1
- tgt_points: bfloat16 [32768, 512], P(('tgt', 'src')), may hold values from -0.5 to 0.5
- tgt_start: float32 [32768], P('tgt'), may hold values from -2 to 10
Outputs:
- src_potential: float32 [16384], P('src')
- tgt_potential: float32 [32768], P('tgt')
The draws below stay inside these ranges and needn't reach their ends.
All inputs are finite; a program needn't handle non-finite values.
Results may differ from the reference program's by a relative error of at most 0.0003.
Values may be sent and summed in bfloat16 or wider, within the bound.
No kernel may reach another device: no remote copies, remote signals or barrier semaphores. Data moves between devices by JAX's collectives and lax.ppermute only.
A program may use at most 64 MiB of HBM per device.

```python
import math
import jax
import jax.numpy as jnp
from jax import lax

DIM = 512
ITERS = 2
NS = 16384
NT = 32768


def planting(key):
    base_key = jax.random.fold_in(key, 101)
    pair_count = NS // 2
    target_pairs = NT // 2
    chosen = jax.random.randint(jax.random.fold_in(base_key, 1), (pair_count,), 0, 8) == 0
    partner = jax.random.randint(jax.random.fold_in(base_key, 2), (pair_count,), 0, target_pairs)
    marked = jnp.zeros((target_pairs,), jnp.int32).at[partner].max(chosen.astype(jnp.int32)) > 0
    spread = jnp.exp(jax.random.uniform(jax.random.fold_in(base_key, 3), (target_pairs, 1), jnp.float32, math.log(0.1), math.log(0.25)))
    anchor = jnp.clip(jax.random.normal(jax.random.fold_in(base_key, 4), (target_pairs, DIM), jnp.float32) * spread, -0.5, 0.5)
    return (chosen, partner, marked, anchor)


def draw_src_points(key, part):
    chosen, partner, marked, anchor = planting(key)
    key = jax.random.fold_in(key, 11)
    key_rows = jax.random.fold_in(key, 1)
    key_vals = jax.random.fold_in(key, 2)
    key_power = jax.random.fold_in(key, 3)
    key_noise = jax.random.fold_in(key, 4)
    lift = jax.random.uniform(key_rows, (NS, 1), jnp.float32)
    values = jax.random.normal(key_vals, (NS, DIM), jnp.float32)
    factor = jnp.exp(lift * math.log(3.5)) / math.sqrt(DIM)
    drawn = jnp.clip(values * factor, -1.0, 1.0)
    pair_count = NS // 2
    power = 1.2 + jax.random.uniform(key_power, (pair_count, 1, 1), jnp.float32)
    aligned = anchor[partner]
    noise = 0.02 * jax.random.normal(key_noise, (pair_count, 2, DIM), jnp.float32)
    planted = jnp.clip(power * aligned[:, None, :] + noise, -1.0, 1.0).reshape(NS, DIM)
    flags = jnp.repeat(chosen, 2)[:, None]
    return jnp.where(flags, planted, drawn).astype(jnp.bfloat16)


def draw_tgt_points(key, part):
    chosen, partner, marked, anchor = planting(key)
    key = jax.random.fold_in(key, 17)
    key_vals = jax.random.fold_in(key, 1)
    key_twin = jax.random.fold_in(key, 2)
    drawn = jnp.clip(0.0625 * jax.random.normal(key_vals, (NT, DIM), jnp.float32), -0.5, 0.5)
    twin = jnp.clip(anchor + 0.005 * jax.random.normal(key_twin, anchor.shape, jnp.float32), -0.5, 0.5)
    planted = jnp.stack([anchor, twin], axis=1).reshape(NT, DIM)
    flags = jnp.repeat(marked, 2)[:, None]
    return jnp.where(flags, planted, drawn).astype(jnp.bfloat16)


def draw_tgt_start(key, part):
    chosen, partner, marked, anchor = planting(key)
    key = jax.random.fold_in(key, 23)
    key_unit = jax.random.fold_in(key, 1)
    key_gap = jax.random.fold_in(key, 2)
    unit = jax.random.uniform(key_unit, (NT,), jnp.float32)
    start = unit * 12.0 - 2.0
    pairs = start.reshape(NT // 2, 2)
    first = pairs[:, 0]
    gap = 0.05 + 0.1 * jax.random.uniform(key_gap, (NT // 2,), jnp.float32)
    second = jnp.where(first < 9.8, first + gap, first - gap)
    second = jnp.where(marked, second, pairs[:, 1])
    return jnp.stack([first, second], axis=1).reshape(NT)


def setup_inputs(seed: int = 0) -> dict:
    streams_of = jax.random.split(jax.random.key(seed), 4)
    return {
        "src_points": draw_src_points(jax.random.fold_in(streams_of[3], 71), 0),
        "tgt_points": draw_tgt_points(jax.random.fold_in(streams_of[3], 71), 0),
        "tgt_start": draw_tgt_start(jax.random.fold_in(streams_of[3], 71), 0),
    }


EPSILON = 0.05


def norms(points):
    wide = points.astype(jnp.float32)
    return jnp.sum(wide * wide, axis=1)


def half_step(rows, row_sq, cols, col_sq, pot, count):
    blocks = rows.reshape(-1, 2048 if rows.shape[0] % 2048 == 0 else rows.shape[0], rows.shape[1])
    sq_blocks = row_sq.reshape(blocks.shape[0], blocks.shape[1])

    def one(item):
        block, block_sq = item
        cost = block_sq[:, None] + col_sq[None, :] - 2.0 * jnp.dot(block, cols.T, preferred_element_type=jnp.float32)
        score = (pot[None, :] - cost) / EPSILON
        peak = jnp.max(score, axis=1)
        total = jnp.sum(jnp.exp(score - peak[:, None]), axis=1)
        return -EPSILON * (peak + jnp.log(total)) + EPSILON * jnp.log(jnp.asarray(count, jnp.float32))

    return lax.map(one, (blocks, sq_blocks)).reshape(-1)


def reference(src_points, tgt_points, tgt_start):
    sx = norms(src_points)
    sy = norms(tgt_points)
    pot_g = tgt_start
    pot_f = jnp.zeros_like(sx)
    for step in range(ITERS):
        pot_f = half_step(src_points, sx, tgt_points, sy, pot_g, NT)
        pot_g = half_step(tgt_points, sy, src_points, sx, pot_f, NS)
    return pot_f, pot_g
```

```python
import functools
import itertools
import math

import jax
import jax.numpy as jnp
from jax import lax
from jax.experimental import pallas as pl
from jax.experimental.pallas import tpu as pltpu
from jax.sharding import PartitionSpec as P

ITERS = 2


EPSILON = 0.05
UNIT = EPSILON

LANES = 128
SUB = 8
VMEM_LIMIT = 16 * 1024 * 1024


def tree(op, values):
    values = list(values)
    while len(values) > 1:
        values = [
            op(values[i], values[i + 1]) if i + 1 < len(values) else values[i]
            for i in range(0, len(values), 2)
        ]
    return values[0]


def merge(peaks, totals):
    peak = jnp.max(peaks, axis=0, keepdims=True)
    return peak + jnp.log(jnp.sum(totals * jnp.exp(peaks - peak), axis=0, keepdims=True))


def merge_parts(parts_ref, count, out_ref):
    parts = [parts_ref[i] for i in range(parts_ref.shape[0])]
    peak = tree(jnp.maximum, parts)
    total = tree(jnp.add, [jnp.exp(part - peak) for part in parts])
    out_ref[...] = math.log(count) - (peak + jnp.log(total))


def repeat(part_ref, part):
    for copy in range(part_ref.shape[0]):
        part_ref[copy] = part


def stacked(first, second):
    return jnp.concatenate([first, second], axis=0)


def power_sum(tiles, peak):
    both = [
        jnp.exp(stacked(tiles[i] - peak, tiles[i + 1] - peak).astype(jnp.bfloat16))
        for i in range(0, len(tiles), 2)
    ]
    total = tree(jnp.add, both).astype(jnp.float32)
    return total[:SUB] + total[SUB:]


def lane_tiles(rows):
    return [rows[:, k : k + LANES] for k in range(0, rows.shape[1], LANES)]


def row_part(load, pots):
    peaks, totals = [], []
    for first in range(0, LANES, SUB):
        tiles = [tile + pot for tile, pot in zip(lane_tiles(load(first)), pots)]
        peak = tree(jnp.maximum, tiles)
        peaks.append(peak)
        totals.append(power_sum(tiles, peak))
    return merge(jnp.concatenate(peaks, axis=0).T, jnp.concatenate(totals, axis=0).T)


def pot_rows(pot_ref):
    return [
        jnp.broadcast_to(pot_ref[k : k + 1, :], (SUB, LANES)) for k in range(pot_ref.shape[0])
    ]


def squares(points):
    wide = points.astype(jnp.float32)
    return jnp.sum(tree(jnp.add, lane_tiles(wide * wide)).T, axis=0, keepdims=True)


def place_kernel(
    own_ref, other_ref, side_ref, side_other_ref, far_ref, theirs_ref, theirs_far_ref, start_ref, targets, sq_ref, pot_ref
):
    own = lax.axis_index("src")
    core = own % 2
    size = own_ref.shape[0]
    chips = targets.shape[0] // (2 * size)

    def put(points, chip, core):
        index = (own // 2 + chip + chips) % chips * 2 + core
        targets[pl.ds(pl.multiple_of(index * size, size), size), :] = points
        per = size // LANES
        for sub in range(per):
            row = squares(points[sub * LANES : (sub + 1) * LANES])
            sq_ref[pl.ds(index * per + sub, 1), :] = row

    side = 2 * core - 1
    put(own_ref[...], 0, core)
    put(other_ref[...], 0, 1 - core)
    put(side_ref[...], side, core)
    put(side_other_ref[...], side, 1 - core)
    put(far_ref[...], 2, core)
    put(theirs_ref[:size, :], -side, 1 - core)
    put(theirs_ref[size:, :], -side, core)
    put(theirs_far_ref[...], 2, 1 - core)
    pot_ref[...] = (start_ref[...] - sq_ref[...]) * (1.0 / UNIT)


def bring_kernel(*refs):
    count = len(refs) // 3
    copies = [
        pltpu.make_async_copy(refs[i], refs[count + i], refs[2 * count + i]) for i in range(count)
    ]
    for copy in copies:
        copy.start()
    for copy in copies:
        copy.wait()


def block_pipeline(points_ref, index_of, tgt_ref, pot_ref, score_ref, rows_ref, sq_ref, even, odd):
    step = even.shape[0]
    per = step // LANES
    steps = points_ref.shape[0] // step

    def product(block, held):
        points = points_ref[pl.ds(pl.multiple_of(block * step, step), step), :]
        tile = lax.dot_general(
            points, tgt_ref[...], (((1,), (1,)), ((), ())), preferred_element_type=jnp.float32
        ) * (2.0 / UNIT)
        held[...] = tile
        for sub in range(per):
            part = slice(sub * LANES, (sub + 1) * LANES)
            index = index_of(block * per + sub)
            score_ref[pl.ds(pl.multiple_of(index * LANES, LANES), LANES), :] = tile[part]
            sq_ref[pl.ds(index, 1), :] = squares(points[part])

    def reduce(held):
        pots = pot_rows(pot_ref)

        def load(start):
            return lambda first: held[start + first : start + first + SUB, :]

        return [row_part(load(sub * LANES), pots) for sub in range(per)]

    def keep(block, rows):
        for sub, row in enumerate(rows):
            rows_ref[pl.ds(index_of(block * per + sub), 1), :] = row

    product(0, even)

    if steps > 2:

        @pl.loop(0, steps // 2 - 1)
        def _(pair):
            rows = reduce(even)
            product(2 * pair + 1, odd)
            keep(2 * pair, rows)
            rows = reduce(odd)
            product(2 * pair + 2, even)
            keep(2 * pair + 1, rows)

    rows = reduce(even)
    product(steps - 1, odd)
    keep(steps - 2, rows)
    keep(steps - 1, reduce(odd))


def row_index(lines):
    own, core = lax.axis_index("tgt"), lax.axis_index("src") % 2
    y, x = own // 4, own % 4
    line, place = y + core * (x - y), x + core * (y - x)

    def index_of(block):
        shift = lines[0] if len(lines) == 1 else lines[0] + block // 4 * (lines[1] - lines[0])
        to_line, to_place = (line + shift + 4) % 4, (place + block % 4 + 3) % 4
        return to_line * (4 - 3 * core) + to_place * (1 + 3 * core)

    return index_of


def own_kernel(points_ref, tgt_ref, pot_ref, score_ref, rows_ref, src_sq_ref, even, odd):
    block_pipeline(
        points_ref, row_index((0,)), tgt_ref, pot_ref, score_ref, rows_ref, src_sq_ref, even, odd
    )


def more_kernel(
    lines, score_in_ref, rows_in_ref, src_sq_in_ref, first_ref, second_ref, tgt_ref, pot_ref,
    score_ref, part_ref, src_sq_ref, rows_ref, points, even, odd,
):
    rows_ref[...] = rows_in_ref[...]
    src_sq_ref[...] = src_sq_in_ref[...]
    half = first_ref.shape[0]
    points[:half, :] = first_ref[...]
    points[half:, :] = second_ref[...]
    block_pipeline(
        points, row_index(lines), tgt_ref, pot_ref, score_ref, rows_ref, src_sq_ref, even, odd
    )
    repeat(part_ref, rows_ref[...])


def two_by_two(blocks, step):
    step(1, False)

    @pl.loop(1, blocks // 2)
    def _(pair):
        step(2 * pair, True)
        step(2 * pair + 1, False)


def row_kernel(count, score_ref, parts_ref, part_ref, pot_ref, rows_ref, *held):
    merge_parts(parts_ref, count, pot_ref)
    pots = pot_rows(pot_ref)
    blocks = score_ref.shape[0] // LANES
    even, odd = held[:2], held[2:]

    def reduce(block, into):
        peaks, totals = into
        start = pl.multiple_of(block * LANES, LANES)
        for first in range(0, LANES, SUB):
            loaded = score_ref[pl.ds(start + first, SUB), :]
            tiles = [tile + pot for tile, pot in zip(lane_tiles(loaded), pots)]
            peak = tree(jnp.maximum, tiles)
            peaks[first : first + SUB, :] = peak
            totals[first : first + SUB, :] = power_sum(tiles, peak)

    def finish(block, held):
        rows_ref[pl.ds(block, 1), :] = merge(held[0][...].T, held[1][...].T)

    def step(block, is_even):
        finish(block - 1, odd if is_even else even)
        reduce(block, even if is_even else odd)

    reduce(0, even)
    two_by_two(blocks, step)
    finish(blocks - 1, odd)
    repeat(part_ref, rows_ref[...])


def col_kernel(
    count, score_ref, parts_ref, sq_ref, pot_out_ref, part_ref, pot_ref, peaks, totals, even, odd
):
    merge_parts(parts_ref, count, pot_ref)
    pot_out_ref[...] = pot_ref[...] * UNIT + sq_ref[...]
    rows, cols = score_ref.shape
    blocks = rows // LANES

    def widen(block, into):
        into[...] = jnp.broadcast_to(pot_ref[pl.ds(block, 1), :], (LANES, LANES)).T

    def reduce(block, wide):
        here = pl.ds(pl.multiple_of(block * LANES, LANES), LANES)
        there = pl.ds(pl.multiple_of(block * SUB, SUB), SUB)
        pots = wide[...]
        for k in range(cols // LANES):
            lanes = slice(k * LANES, (k + 1) * LANES)
            tile = score_ref[here, lanes] + pots
            tiles = [tile[i : i + SUB] for i in range(0, LANES, SUB)]
            peak = tree(jnp.maximum, tiles)
            peaks[there, lanes] = peak
            totals[there, lanes] = power_sum(tiles, peak)

    def step(block, is_even):
        widen(block, even if is_even else odd)
        reduce(block - 1, odd if is_even else even)

    widen(0, even)
    two_by_two(blocks, step)
    reduce(blocks - 1, odd)
    for k in range(cols // LANES):
        lanes = slice(k * LANES, (k + 1) * LANES)
        pot_ref[k : k + 1, :] = merge(peaks[:, lanes], totals[:, lanes])
    repeat(part_ref, pot_ref[...])


def last_kernel(count, parts_ref, sq_ref, out_ref):
    merge_parts(parts_ref, count, out_ref)
    out_ref[...] = out_ref[...] * UNIT + sq_ref[...]


def params():
    return pltpu.CompilerParams(vmem_limit_bytes=VMEM_LIMIT)


def vec(size):
    return jax.ShapeDtypeStruct((size // LANES, LANES), jnp.float32)


def vecs(copies, size):
    return jax.ShapeDtypeStruct((copies, size // LANES, LANES), jnp.float32)


def scratch(*shape):
    return pltpu.VMEM(shape, jnp.float32)


ANYWHERE = pl.BlockSpec(memory_space=pl.ANY)
IN_VMEM = pl.BlockSpec(memory_space=pltpu.VMEM)


def place(own, other, side, side_other, far, theirs, theirs_far, start):
    rows, width = 8 * own.shape[0], own.shape[1]
    return pl.pallas_call(
        place_kernel,
        out_shape=(pltpu.VMEM((rows, width), own.dtype), vec(rows), vec(rows)),
        in_specs=[IN_VMEM] * 8,
        out_specs=(IN_VMEM,) * 3,
        cost_estimate=cost(rows, width, 1),
        compiler_params=params(),
        name="place",
    )(own, other, side, side_other, far, theirs, theirs_far, start)


def bring(*arrays):
    return pl.pallas_call(
        bring_kernel,
        out_shape=tuple(pltpu.VMEM(a.shape, a.dtype) for a in arrays),
        in_specs=[pl.BlockSpec(memory_space=pltpu.HBM)] * len(arrays),
        out_specs=(IN_VMEM,) * len(arrays),
        scratch_shapes=[pltpu.SemaphoreType.DMA] * len(arrays),
        compiler_params=params(),
        name="bring",
    )(*[pltpu.with_memory_space_constraint(a, pltpu.HBM) for a in arrays])


def cost(rows, cols, width):
    return pl.CostEstimate(
        flops=2 * rows * cols * width, bytes_accessed=8 * rows * cols, transcendentals=rows * cols
    )


def own_pass(points, targets, pot, rows):
    cols, width = targets.shape
    return pl.pallas_call(
        own_kernel,
        out_shape=(pltpu.VMEM((rows, cols), jnp.float32), vec(rows), vec(rows)),
        in_specs=[IN_VMEM] * 3,
        out_specs=(IN_VMEM,) * 3,
        scratch_shapes=[scratch(256, cols)] * 2,
        cost_estimate=cost(points.shape[0], cols, width),
        compiler_params=params(),
        name="own_pass",
    )(points, targets, pot)


def more_pass(state, first, second, lines, targets, pot, copies):
    score, row_parts, src_sq = state
    (rows, cols), width = score.shape, targets.shape[1]
    points = 2 * first.shape[0]
    score = pltpu.with_memory_space_constraint(score, pltpu.VMEM)
    return pl.pallas_call(
        functools.partial(more_kernel, lines),
        out_shape=(pltpu.VMEM((rows, cols), jnp.float32), vecs(copies, rows), vec(rows)),
        in_specs=[IN_VMEM] * 7,
        out_specs=(IN_VMEM,) * 3,
        scratch_shapes=[scratch(rows // LANES, LANES), pltpu.VMEM((points, width), first.dtype)]
        + [scratch(256, cols)] * 2,
        input_output_aliases={0: 0},
        cost_estimate=cost(points, cols, width),
        compiler_params=params(),
        name="more_pass",
    )(score, row_parts, src_sq, first, second, targets, pot)


def row_pass_call(score, parts, count, copies):
    rows, cols = score.shape
    return pl.pallas_call(
        functools.partial(row_kernel, count),
        out_shape=vecs(copies, rows),
        in_specs=[IN_VMEM] * 2,
        out_specs=IN_VMEM,
        scratch_shapes=[scratch(cols // LANES, LANES), scratch(rows // LANES, LANES)]
        + [scratch(LANES, LANES)] * 4,
        compiler_params=params(),
        name="row_pass",
    )(score, parts)


def col_pass_call(score, parts, sq, count, copies):
    rows, cols = score.shape
    return pl.pallas_call(
        functools.partial(col_kernel, count),
        out_shape=(vec(rows), vecs(copies, cols)),
        in_specs=[IN_VMEM] * 3,
        out_specs=(IN_VMEM, IN_VMEM),
        scratch_shapes=[scratch(max(rows, cols) // LANES, LANES)]
        + [scratch(rows // LANES * SUB, cols)] * 2
        + [scratch(LANES, LANES)] * 2,
        compiler_params=params(),
        name="col_pass",
    )(score, parts, sq)


def last_call(parts, sq, count):
    return pl.pallas_call(
        functools.partial(last_kernel, count),
        out_shape=jax.ShapeDtypeStruct(sq.shape, jnp.float32),
        in_specs=[IN_VMEM] * 2,
        out_specs=IN_VMEM,
        compiler_params=params(),
        name="last",
    )(parts, sq)


def exchange(part, axis):
    return lax.all_to_all(part, axis, 0, 0, tiled=True)


def move(block, to):
    pairs = []
    for z, core, y, x in itertools.product(range(4), range(2), range(4), range(4)):
        a, b, c, d = to(z, core, y, x)
        pairs.append((((z * 2 + core) * 4 + y) * 4 + x, ((a % 4 * 2 + b) * 4 + c % 4) * 4 + d % 4))
    return lax.ppermute(block, ("src", "tgt"), pairs)


def other_core(block):
    return move(block, lambda z, core, y, x: (z, 1 - core, y, x))


def round_z(block):
    return move(block, lambda z, core, y, x: (z + 1 - 2 * core, core, y, x))


def along_line(block, by):
    return move(block, lambda z, core, y, x: (z, core, y + core * by, x + (1 - core) * by))


def across_lines(block, by):
    return move(block, lambda z, core, y, x: (z, core, y + (1 - core) * by, x + core * by))


def after(value, earlier):
    def kernel(*refs):
        del refs

    return pl.pallas_call(
        kernel,
        out_shape=jax.ShapeDtypeStruct(value.shape, value.dtype),
        in_specs=[ANYWHERE] * 2,
        out_specs=ANYWHERE,
        input_output_aliases={0: 0},
        cost_estimate=pl.CostEstimate(flops=0, bytes_accessed=40_000_000, transcendentals=0),
        compiler_params=params(),
        name="after",
    )(value, earlier)


def gather_targets(own, earlier):
    side = round_z(own)
    other = other_core(own)
    far = round_z(after(side, earlier))
    side_other = round_z(other)
    theirs = other_core(jnp.concatenate([side, side_other]))
    return other, side, side_other, far, theirs, other_core(far)


def local(src_points, tgt_points, tgt_start):
    n_src, n_tgt = lax.axis_size("src"), lax.axis_size("tgt")
    own, size = src_points, src_points.shape[0]
    total_src = size * n_tgt * n_src
    total_tgt = tgt_points.shape[0] * n_src * n_tgt
    held, tgt_held, start = bring(own, tgt_points, tgt_start.reshape(-1, LANES))

    line = jnp.concatenate([along_line(own, 1), held, along_line(own, -1), along_line(own, 2)])
    before, behind = across_lines(line, 1), across_lines(line, -1)
    far_low, far_high = across_lines(before[: 2 * size], 1), across_lines(behind[2 * size :], -1)

    targets, tgt_sq, red_g = place(tgt_held, *gather_targets(tgt_points, line), start)
    targets = pltpu.with_memory_space_constraint(targets, pltpu.VMEM)
    state = own_pass(line, targets, red_g, size * n_tgt)
    score, part, src_sq = more_pass(state, before, behind, (-1, 1), targets, red_g, 1)
    state = score, part[0], src_sq
    score, part, src_sq = more_pass(state, far_low, far_high, (2,), targets, red_g, n_tgt)
    score = pltpu.with_memory_space_constraint(score, pltpu.VMEM)
    for step in range(ITERS):
        if step:
            part = row_pass_call(score, parts, total_src, n_tgt)
        parts = exchange(part, "tgt")
        pot_f, part = col_pass_call(score, parts, src_sq, total_tgt, n_src)
        parts = exchange(part, "src")
    pot_g = last_call(parts, tgt_sq, total_src)
    return (pot_f.reshape(-1), pot_g.reshape(-1))


def solution(mesh):
    return jax.shard_map(
        local,
        mesh=mesh,
        in_specs=(P(("src", "tgt"), None), P(("tgt", "src"), None), P("tgt")),
        out_specs=(P("src"), P("tgt")),
        check_vma=False,
    )
```

```python
import functools
import itertools
import math

import jax
import jax.numpy as jnp
from jax import lax
from jax.experimental import pallas as pl
from jax.experimental.pallas import tpu as pltpu
from jax.sharding import PartitionSpec as P

ITERS = 2


EPSILON = 0.05
UNIT = EPSILON

LANES = 128
SUB = 8
VMEM_LIMIT = 16 * 1024 * 1024


def tree(op, values):
    values = list(values)
    while len(values) > 1:
        values = [
            op(values[i], values[i + 1]) if i + 1 < len(values) else values[i]
            for i in range(0, len(values), 2)
        ]
    return values[0]


def merge(peaks, totals):
    peak = jnp.max(peaks, axis=0, keepdims=True)
    return peak + jnp.log(jnp.sum(totals * jnp.exp(peaks - peak), axis=0, keepdims=True))


def merge_parts(parts_ref, count, out_ref):
    parts = [parts_ref[i] for i in range(parts_ref.shape[0])]
    peak = tree(jnp.maximum, parts)
    total = tree(jnp.add, [jnp.exp(part - peak) for part in parts])
    out_ref[...] = math.log(count) - (peak + jnp.log(total))


def repeat(part_ref, part):
    for copy in range(part_ref.shape[0]):
        part_ref[copy] = part


def stacked(first, second):
    return jnp.concatenate([first, second], axis=0)


def power_sum(tiles, peak):
    both = [
        jnp.exp(stacked(tiles[i] - peak, tiles[i + 1] - peak).astype(jnp.bfloat16))
        for i in range(0, len(tiles), 2)
    ]
    total = tree(jnp.add, both).astype(jnp.float32)
    return total[:SUB] + total[SUB:]


def lane_tiles(rows):
    return [rows[:, k : k + LANES] for k in range(0, rows.shape[1], LANES)]


def row_part(load, pots):
    peaks, totals = [], []
    for first in range(0, LANES, SUB):
        tiles = [tile + pot for tile, pot in zip(lane_tiles(load(first)), pots)]
        peak = tree(jnp.maximum, tiles)
        peaks.append(peak)
        totals.append(power_sum(tiles, peak))
    return merge(jnp.concatenate(peaks, axis=0).T, jnp.concatenate(totals, axis=0).T)


def pot_rows(pot_ref):
    return [
        jnp.broadcast_to(pot_ref[k : k + 1, :], (SUB, LANES)) for k in range(pot_ref.shape[0])
    ]


def squares(points):
    wide = points.astype(jnp.float32)
    return jnp.sum(tree(jnp.add, lane_tiles(wide * wide)).T, axis=0, keepdims=True)


def place_kernel(
    own_ref, other_ref, side_ref, side_other_ref, far_ref, theirs_ref, theirs_far_ref, start_ref, targets, sq_ref, pot_ref
):
    own = lax.axis_index("src")
    core = own % 2
    size = own_ref.shape[0]
    chips = targets.shape[0] // (2 * size)

    def put(points, chip, core):
        index = (own // 2 + chip + chips) % chips * 2 + core
        targets[pl.ds(pl.multiple_of(index * size, size), size), :] = points
        per = size // LANES
        for sub in range(per):
            row = squares(points[sub * LANES : (sub + 1) * LANES])
            sq_ref[pl.ds(index * per + sub, 1), :] = row

    side = 2 * core - 1
    put(own_ref[...], 0, core)
    put(other_ref[...], 0, 1 - core)
    put(side_ref[...], side, core)
    put(side_other_ref[...], side, 1 - core)
    put(far_ref[...], 2, core)
    put(theirs_ref[:size, :], -side, 1 - core)
    put(theirs_ref[size:, :], -side, core)
    put(theirs_far_ref[...], 2, 1 - core)
    pot_ref[...] = (start_ref[...] - sq_ref[...]) * (1.0 / UNIT)


def bring_kernel(*refs):
    count = len(refs) // 3
    copies = [
        pltpu.make_async_copy(refs[i], refs[count + i], refs[2 * count + i]) for i in range(count)
    ]
    for copy in copies:
        copy.start()
    for copy in copies:
        copy.wait()


CHUNK = 256


def block_pipeline(points_ref, index_of, tgt_ref, pot_ref, score_ref, rows_ref, sq_ref, held, peaks, totals):
    step, cols = held[0].shape
    per = step // LANES
    steps = points_ref.shape[0] // step
    chunks = cols // CHUNK
    pots = pot_rows(pot_ref)

    def product(at, chunk):
        points = points_ref[at * step : (at + 1) * step, :]
        lanes = slice(chunk * CHUNK, (chunk + 1) * CHUNK)
        tile = lax.dot_general(
            points, tgt_ref[lanes, :], (((1,), (1,)), ((), ())), preferred_element_type=jnp.float32
        ) * (2.0 / UNIT)
        held[at % 2][:, lanes] = tile
        for sub in range(per):
            part = slice(sub * LANES, (sub + 1) * LANES)
            index = index_of(at * per + sub)
            score_ref[pl.ds(pl.multiple_of(index * LANES, LANES), LANES), lanes] = tile[part]
            if chunk == sub:
                sq_ref[pl.ds(index, 1), :] = squares(points[part])

    def reduce(at, chunk):
        size = step // chunks
        for first in range(chunk * size, (chunk + 1) * size, SUB):
            rows = slice(first, first + SUB)
            tiles = [tile + pot for tile, pot in zip(lane_tiles(held[at % 2][rows, :]), pots)]
            peak = tree(jnp.maximum, tiles)
            peaks[at % 2][rows, :] = peak
            totals[at % 2][rows, :] = power_sum(tiles, peak)

    def finish(at):
        for sub in range(per):
            part = slice(sub * LANES, (sub + 1) * LANES)
            row = merge(peaks[at % 2][part, :].T, totals[at % 2][part, :].T)
            rows_ref[pl.ds(index_of(at * per + sub), 1), :] = row

    for chunk in range(chunks):
        product(0, chunk)
    for at in range(steps):
        for chunk in range(chunks):
            if at + 1 < steps:
                product(at + 1, chunk)
            reduce(at, chunk)
            if at and chunk == chunks // 2:
                finish(at - 1)
    finish(steps - 1)


def row_index(lines):
    own, core = lax.axis_index("tgt"), lax.axis_index("src") % 2
    y, x = own // 4, own % 4
    line, place = y + core * (x - y), x + core * (y - x)

    def index_of(block):
        shift = lines[0] if len(lines) == 1 else lines[0] + block // 4 * (lines[1] - lines[0])
        to_line, to_place = (line + shift + 4) % 4, (place + block % 4 + 3) % 4
        return to_line * (4 - 3 * core) + to_place * (1 + 3 * core)

    return index_of


def own_kernel(points_ref, tgt_ref, pot_ref, score_ref, rows_ref, src_sq_ref, *held):
    block_pipeline(
        points_ref, row_index((0,)), tgt_ref, pot_ref, score_ref, rows_ref, src_sq_ref,
        held[:2], held[2:4], held[4:],
    )


def more_kernel(
    lines, score_in_ref, rows_in_ref, src_sq_in_ref, first_ref, second_ref, tgt_ref, pot_ref,
    score_ref, part_ref, src_sq_ref, rows_ref, points, *held,
):
    rows_ref[...] = rows_in_ref[...]
    src_sq_ref[...] = src_sq_in_ref[...]
    half = first_ref.shape[0]
    points[:half, :] = first_ref[...]
    points[half:, :] = second_ref[...]
    block_pipeline(
        points, row_index(lines), tgt_ref, pot_ref, score_ref, rows_ref, src_sq_ref,
        held[:2], held[2:4], held[4:],
    )
    repeat(part_ref, rows_ref[...])


def two_by_two(blocks, step):
    step(1, False)

    @pl.loop(1, blocks // 2)
    def _(pair):
        step(2 * pair, True)
        step(2 * pair + 1, False)


def row_kernel(count, score_ref, parts_ref, part_ref, pot_ref, rows_ref, *held):
    merge_parts(parts_ref, count, pot_ref)
    pots = pot_rows(pot_ref)
    blocks = score_ref.shape[0] // LANES
    even, odd = held[:2], held[2:]

    def reduce(block, into):
        peaks, totals = into
        start = pl.multiple_of(block * LANES, LANES)
        for first in range(0, LANES, SUB):
            loaded = score_ref[pl.ds(start + first, SUB), :]
            tiles = [tile + pot for tile, pot in zip(lane_tiles(loaded), pots)]
            peak = tree(jnp.maximum, tiles)
            peaks[first : first + SUB, :] = peak
            totals[first : first + SUB, :] = power_sum(tiles, peak)

    def finish(block, held):
        rows_ref[pl.ds(block, 1), :] = merge(held[0][...].T, held[1][...].T)

    def step(block, is_even):
        finish(block - 1, odd if is_even else even)
        reduce(block, even if is_even else odd)

    reduce(0, even)
    two_by_two(blocks, step)
    finish(blocks - 1, odd)
    repeat(part_ref, rows_ref[...])


def col_kernel(
    count, score_ref, parts_ref, sq_ref, pot_out_ref, part_ref, pot_ref, peaks, totals, even, odd
):
    merge_parts(parts_ref, count, pot_ref)
    pot_out_ref[...] = pot_ref[...] * UNIT + sq_ref[...]
    rows, cols = score_ref.shape
    blocks = rows // LANES

    def widen(block, into):
        into[...] = jnp.broadcast_to(pot_ref[pl.ds(block, 1), :], (LANES, LANES)).T

    def reduce(block, wide):
        here = pl.ds(pl.multiple_of(block * LANES, LANES), LANES)
        there = pl.ds(pl.multiple_of(block * SUB, SUB), SUB)
        pots = wide[...]
        for k in range(cols // LANES):
            lanes = slice(k * LANES, (k + 1) * LANES)
            tile = score_ref[here, lanes] + pots
            tiles = [tile[i : i + SUB] for i in range(0, LANES, SUB)]
            peak = tree(jnp.maximum, tiles)
            peaks[there, lanes] = peak
            totals[there, lanes] = power_sum(tiles, peak)

    def step(block, is_even):
        widen(block, even if is_even else odd)
        reduce(block - 1, odd if is_even else even)

    widen(0, even)
    two_by_two(blocks, step)
    reduce(blocks - 1, odd)
    for k in range(cols // LANES):
        lanes = slice(k * LANES, (k + 1) * LANES)
        pot_ref[k : k + 1, :] = merge(peaks[:, lanes], totals[:, lanes])
    repeat(part_ref, pot_ref[...])


def last_kernel(count, parts_ref, sq_ref, out_ref):
    merge_parts(parts_ref, count, out_ref)
    out_ref[...] = out_ref[...] * UNIT + sq_ref[...]


def params():
    return pltpu.CompilerParams(vmem_limit_bytes=VMEM_LIMIT)


def vec(size):
    return jax.ShapeDtypeStruct((size // LANES, LANES), jnp.float32)


def vecs(copies, size):
    return jax.ShapeDtypeStruct((copies, size // LANES, LANES), jnp.float32)


def scratch(*shape):
    return pltpu.VMEM(shape, jnp.float32)


ANYWHERE = pl.BlockSpec(memory_space=pl.ANY)
IN_VMEM = pl.BlockSpec(memory_space=pltpu.VMEM)


def place(own, other, side, side_other, far, theirs, theirs_far, start):
    rows, width = 8 * own.shape[0], own.shape[1]
    return pl.pallas_call(
        place_kernel,
        out_shape=(pltpu.VMEM((rows, width), own.dtype), vec(rows), vec(rows)),
        in_specs=[IN_VMEM] * 8,
        out_specs=(IN_VMEM,) * 3,
        cost_estimate=cost(rows, width, 1),
        compiler_params=params(),
        name="place",
    )(own, other, side, side_other, far, theirs, theirs_far, start)


def bring(*arrays):
    return pl.pallas_call(
        bring_kernel,
        out_shape=tuple(pltpu.VMEM(a.shape, a.dtype) for a in arrays),
        in_specs=[pl.BlockSpec(memory_space=pltpu.HBM)] * len(arrays),
        out_specs=(IN_VMEM,) * len(arrays),
        scratch_shapes=[pltpu.SemaphoreType.DMA] * len(arrays),
        compiler_params=params(),
        name="bring",
    )(*[pltpu.with_memory_space_constraint(a, pltpu.HBM) for a in arrays])


def cost(rows, cols, width):
    return pl.CostEstimate(
        flops=2 * rows * cols * width, bytes_accessed=8 * rows * cols, transcendentals=rows * cols
    )


STEP = 256


def step_scratch(cols):
    return [scratch(STEP, cols)] * 2 + [scratch(STEP, LANES)] * 4


def own_pass(points, targets, pot, rows):
    cols, width = targets.shape
    return pl.pallas_call(
        own_kernel,
        out_shape=(pltpu.VMEM((rows, cols), jnp.float32), vec(rows), vec(rows)),
        in_specs=[IN_VMEM] * 3,
        out_specs=(IN_VMEM,) * 3,
        scratch_shapes=step_scratch(cols),
        cost_estimate=cost(points.shape[0], cols, width),
        compiler_params=params(),
        name="own_pass",
    )(points, targets, pot)


def more_pass(state, first, second, lines, targets, pot, copies):
    score, row_parts, src_sq = state
    (rows, cols), width = score.shape, targets.shape[1]
    points = 2 * first.shape[0]
    score = pltpu.with_memory_space_constraint(score, pltpu.VMEM)
    return pl.pallas_call(
        functools.partial(more_kernel, lines),
        out_shape=(pltpu.VMEM((rows, cols), jnp.float32), vecs(copies, rows), vec(rows)),
        in_specs=[IN_VMEM] * 7,
        out_specs=(IN_VMEM,) * 3,
        scratch_shapes=[scratch(rows // LANES, LANES), pltpu.VMEM((points, width), first.dtype)]
        + step_scratch(cols),
        input_output_aliases={0: 0},
        cost_estimate=cost(points, cols, width),
        compiler_params=params(),
        name="more_pass",
    )(score, row_parts, src_sq, first, second, targets, pot)


def row_pass_call(score, parts, count, copies):
    rows, cols = score.shape
    return pl.pallas_call(
        functools.partial(row_kernel, count),
        out_shape=vecs(copies, rows),
        in_specs=[IN_VMEM] * 2,
        out_specs=IN_VMEM,
        scratch_shapes=[scratch(cols // LANES, LANES), scratch(rows // LANES, LANES)]
        + [scratch(LANES, LANES)] * 4,
        compiler_params=params(),
        name="row_pass",
    )(score, parts)


def col_pass_call(score, parts, sq, count, copies):
    rows, cols = score.shape
    return pl.pallas_call(
        functools.partial(col_kernel, count),
        out_shape=(vec(rows), vecs(copies, cols)),
        in_specs=[IN_VMEM] * 3,
        out_specs=(IN_VMEM, IN_VMEM),
        scratch_shapes=[scratch(max(rows, cols) // LANES, LANES)]
        + [scratch(rows // LANES * SUB, cols)] * 2
        + [scratch(LANES, LANES)] * 2,
        compiler_params=params(),
        name="col_pass",
    )(score, parts, sq)


def last_call(parts, sq, count):
    return pl.pallas_call(
        functools.partial(last_kernel, count),
        out_shape=jax.ShapeDtypeStruct(sq.shape, jnp.float32),
        in_specs=[IN_VMEM] * 2,
        out_specs=IN_VMEM,
        compiler_params=params(),
        name="last",
    )(parts, sq)


def exchange(part, axis):
    return lax.all_to_all(part, axis, 0, 0, tiled=True)


def move(block, to):
    pairs = []
    for z, core, y, x in itertools.product(range(4), range(2), range(4), range(4)):
        a, b, c, d = to(z, core, y, x)
        pairs.append((((z * 2 + core) * 4 + y) * 4 + x, ((a % 4 * 2 + b) * 4 + c % 4) * 4 + d % 4))
    return lax.ppermute(block, ("src", "tgt"), pairs)


def other_core(block):
    return move(block, lambda z, core, y, x: (z, 1 - core, y, x))


def round_z(block):
    return move(block, lambda z, core, y, x: (z + 1 - 2 * core, core, y, x))


def along_line(block, by):
    return move(block, lambda z, core, y, x: (z, core, y + core * by, x + (1 - core) * by))


def across_lines(block, by):
    return move(block, lambda z, core, y, x: (z, core, y + (1 - core) * by, x + core * by))


def after(value, earlier):
    def kernel(*refs):
        del refs

    return pl.pallas_call(
        kernel,
        out_shape=jax.ShapeDtypeStruct(value.shape, value.dtype),
        in_specs=[ANYWHERE] * 2,
        out_specs=ANYWHERE,
        input_output_aliases={0: 0},
        cost_estimate=pl.CostEstimate(flops=0, bytes_accessed=40_000_000, transcendentals=0),
        compiler_params=params(),
        name="after",
    )(value, earlier)


def gather_targets(own, earlier):
    side = round_z(own)
    other = other_core(own)
    far = round_z(after(side, earlier))
    side_other = round_z(other)
    theirs = other_core(jnp.concatenate([side, side_other]))
    return other, side, side_other, far, theirs, other_core(far)


def local(src_points, tgt_points, tgt_start):
    n_src, n_tgt = lax.axis_size("src"), lax.axis_size("tgt")
    own, size = src_points, src_points.shape[0]
    total_src = size * n_tgt * n_src
    total_tgt = tgt_points.shape[0] * n_src * n_tgt
    held, tgt_held, start = bring(own, tgt_points, tgt_start.reshape(-1, LANES))

    line = jnp.concatenate([along_line(own, 1), held, along_line(own, -1), along_line(own, 2)])
    before, behind = across_lines(line, 1), across_lines(line, -1)
    far_low, far_high = across_lines(before[: 2 * size], 1), across_lines(behind[2 * size :], -1)

    targets, tgt_sq, red_g = place(tgt_held, *gather_targets(tgt_points, line), start)
    targets = pltpu.with_memory_space_constraint(targets, pltpu.VMEM)
    state = own_pass(line, targets, red_g, size * n_tgt)
    score, part, src_sq = more_pass(state, before, behind, (-1, 1), targets, red_g, 1)
    state = score, part[0], src_sq
    score, part, src_sq = more_pass(state, far_low, far_high, (2,), targets, red_g, n_tgt)
    score = pltpu.with_memory_space_constraint(score, pltpu.VMEM)
    for step in range(ITERS):
        if step:
            part = row_pass_call(score, parts, total_src, n_tgt)
        parts = exchange(part, "tgt")
        pot_f, part = col_pass_call(score, parts, src_sq, total_tgt, n_src)
        parts = exchange(part, "src")
    pot_g = last_call(parts, tgt_sq, total_src)
    return (pot_f.reshape(-1), pot_g.reshape(-1))


def solution(mesh):
    return jax.shard_map(
        local,
        mesh=mesh,
        in_specs=(P(("src", "tgt"), None), P(("tgt", "src"), None), P("tgt")),
        out_specs=(P("src"), P("tgt")),
        check_vma=False,
    )
```

```python
import functools
import itertools
import math

import jax
import jax.numpy as jnp
from jax import lax
from jax.experimental import pallas as pl
from jax.experimental.pallas import tpu as pltpu
from jax.sharding import PartitionSpec as P

ITERS = 2


EPSILON = 0.05
UNIT = EPSILON * math.log(2.0)

LANES = 128
SUB = 8
VMEM_LIMIT = 16 * 1024 * 1024


def tree(op, values):
    values = list(values)
    while len(values) > 1:
        values = [
            op(values[i], values[i + 1]) if i + 1 < len(values) else values[i]
            for i in range(0, len(values), 2)
        ]
    return values[0]


def merge(peaks, totals):
    peak = jnp.max(peaks, axis=0, keepdims=True)
    return peak + jnp.log2(jnp.sum(totals * jnp.exp2(peaks - peak), axis=0, keepdims=True))


def merge_parts(parts_ref, count, out_ref):
    parts = [parts_ref[i] for i in range(parts_ref.shape[0])]
    peak = tree(jnp.maximum, parts)
    total = tree(jnp.add, [jnp.exp2(part - peak) for part in parts])
    out_ref[...] = math.log2(count) - (peak + jnp.log2(total))


def repeat(part_ref, part):
    for copy in range(part_ref.shape[0]):
        part_ref[copy] = part


def power_sum(tiles, peak):
    return tree(jnp.add, [jnp.exp2(tile - peak) for tile in tiles])


def lane_tiles(rows):
    return [rows[:, k : k + LANES] for k in range(0, rows.shape[1], LANES)]


def reduce_rows(score_ref, start, groups, pots, peaks, totals):
    for group in groups:
        rows = pl.ds(start + group * SUB, SUB)
        tiles = [tile + pot for tile, pot in zip(lane_tiles(score_ref[rows, :]), pots)]
        peak = tree(jnp.maximum, tiles)
        at = group * SUB
        peaks[at : at + SUB, :] = peak
        totals[at : at + SUB, :] = power_sum(tiles, peak)


def merge_rows(peaks, totals):
    return merge(peaks[...].T, totals[...].T)


def pot_rows(pot_ref):
    return [
        jnp.broadcast_to(pot_ref[k : k + 1, :], (SUB, LANES)) for k in range(pot_ref.shape[0])
    ]


def squares(points):
    wide = points.astype(jnp.float32)
    return jnp.sum(tree(jnp.add, lane_tiles(wide * wide)).T, axis=0, keepdims=True)


def place_kernel(
    own_ref, other_ref, side_ref, side_other_ref, far_ref, theirs_ref, theirs_far_ref, start_ref, targets, sq_ref, pot_ref
):
    own = lax.axis_index("src")
    core = own % 2
    size = own_ref.shape[0]
    chips = targets.shape[0] // (2 * size)

    def put(points, chip, core):
        index = (own // 2 + chip + chips) % chips * 2 + core
        targets[pl.ds(pl.multiple_of(index * size, size), size), :] = points
        per = size // LANES
        for sub in range(per):
            row = squares(points[sub * LANES : (sub + 1) * LANES])
            sq_ref[pl.ds(index * per + sub, 1), :] = row

    side = 2 * core - 1
    put(own_ref[...], 0, core)
    put(other_ref[...], 0, 1 - core)
    put(side_ref[...], side, core)
    put(side_other_ref[...], side, 1 - core)
    put(far_ref[...], 2, core)
    put(theirs_ref[:size, :], -side, 1 - core)
    put(theirs_ref[size:, :], -side, core)
    put(theirs_far_ref[...], 2, 1 - core)
    pot_ref[...] = (start_ref[...] - sq_ref[...]) * (1.0 / UNIT)


def bring_kernel(*refs):
    count = len(refs) // 3
    copies = [
        pltpu.make_async_copy(refs[i], refs[count + i], refs[2 * count + i]) for i in range(count)
    ]
    for copy in copies:
        copy.start()
    for copy in copies:
        copy.wait()


CHUNK = 256


def row_index(block):
    own, core = lax.axis_index("tgt"), lax.axis_index("src") % 2
    y, x = own // 4, own % 4
    line, place = y + core * (x - y), x + core * (y - x)
    at = block % 4
    by = at + 2 * (at % 2) * (1 - at // 2) - at // 2
    to_line, to_place = (line + block // 4) % 4, (place + by) % 4
    return to_line * (4 - 3 * core) + to_place * (1 + 3 * core)


def block_pipeline(sources, tgt_ref, pot_ref, score_ref, rows_ref, sq_ref, peaks, totals):
    per = STEP // LANES
    chunks = tgt_ref.shape[0] // CHUNK
    pots = pot_rows(pot_ref)

    def product(at, chunk):
        ref, first, block = sources[at]
        points = ref[first : first + STEP, :]
        lanes = slice(chunk * CHUNK, (chunk + 1) * CHUNK)
        score_ref[block * LANES : (block + per) * LANES, lanes] = lax.dot_general(
            points, tgt_ref[lanes, :], (((1,), (1,)), ((), ())), preferred_element_type=jnp.float32
        ) * (2.0 / UNIT)
        if chunk < per:
            row = squares(points[chunk * LANES : (chunk + 1) * LANES])
            sq_ref[pl.ds(row_index(block + chunk), 1), :] = row

    def reduce(at, chunk):
        share = chunks // per
        sub, part = chunk // share, chunk % share
        held = at % 2 * per + sub
        start = (sources[at][2] + sub) * LANES
        size = LANES // SUB // share
        groups = range(part * size, (part + 1) * size)
        reduce_rows(score_ref, start, groups, pots, peaks[held], totals[held])

    def finish(at):
        for sub in range(per):
            held = at % 2 * per + sub
            row = merge_rows(peaks[held], totals[held])
            rows_ref[pl.ds(row_index(sources[at][2] + sub), 1), :] = row

    for chunk in range(chunks):
        product(0, chunk)
    for at in range(len(sources)):
        for chunk in range(chunks):
            if at + 1 < len(sources):
                product(at + 1, chunk)
            reduce(at, chunk)
            if at and chunk == chunks // 2:
                finish(at - 1)
    finish(len(sources) - 1)


def own_kernel(points_ref, tgt_ref, pot_ref, score_ref, rows_ref, src_sq_ref, *held):
    sources = [(points_ref, 0, 0), (points_ref, STEP, 2)]
    block_pipeline(sources, tgt_ref, pot_ref, score_ref, rows_ref, src_sq_ref, held[:4], held[4:])


def more_kernel(
    blocks, score_in_ref, rows_in_ref, src_sq_in_ref, first_ref, second_ref, tgt_ref, pot_ref,
    score_ref, part_ref, src_sq_ref, rows_ref, *held,
):
    rows_ref[...] = rows_in_ref[...]
    src_sq_ref[...] = src_sq_in_ref[...]
    sources = [
        (ref, first, block + first // LANES)
        for ref, block in zip((first_ref, second_ref), blocks)
        for first in range(0, ref.shape[0], STEP)
    ]
    block_pipeline(sources, tgt_ref, pot_ref, score_ref, rows_ref, src_sq_ref, held[:4], held[4:])
    repeat(part_ref, rows_ref[...])


def two_by_two(blocks, step):
    step(1, False)

    @pl.loop(1, blocks // 2)
    def _(pair):
        step(2 * pair, True)
        step(2 * pair + 1, False)


def row_kernel(count, score_ref, parts_ref, part_ref, pot_ref, rows_ref, *held):
    merge_parts(parts_ref, count, pot_ref)
    pots = pot_rows(pot_ref)
    blocks = score_ref.shape[0] // LANES
    even, odd = held[:2], held[2:]

    def reduce(block, into):
        start = pl.multiple_of(block * LANES, LANES)
        reduce_rows(score_ref, start, range(LANES // SUB), pots, *into)

    def finish(block, held):
        rows_ref[pl.ds(row_index(block), 1), :] = merge_rows(*held)

    def step(block, is_even):
        finish(block - 1, odd if is_even else even)
        reduce(block, even if is_even else odd)

    reduce(0, even)
    two_by_two(blocks, step)
    finish(blocks - 1, odd)
    repeat(part_ref, rows_ref[...])


def col_kernel(
    count, score_ref, parts_ref, sq_ref, pot_out_ref, part_ref, pot_ref, peaks, totals, even, odd
):
    merge_parts(parts_ref, count, pot_ref)
    pot_out_ref[...] = pot_ref[...] * UNIT + sq_ref[...]
    rows, cols = score_ref.shape
    blocks = rows // LANES

    def widen(block, into):
        row = pot_ref[pl.ds(row_index(block), 1), :]
        into[...] = jnp.broadcast_to(row, (LANES, LANES)).T

    def reduce(block, wide):
        here = pl.ds(pl.multiple_of(block * LANES, LANES), LANES)
        there = pl.ds(pl.multiple_of(block * SUB, SUB), SUB)
        pots = wide[...]
        for k in range(cols // LANES):
            lanes = slice(k * LANES, (k + 1) * LANES)
            tile = score_ref[here, lanes] + pots
            tiles = [tile[i : i + SUB] for i in range(0, LANES, SUB)]
            peak = tree(jnp.maximum, tiles)
            peaks[there, lanes] = peak
            totals[there, lanes] = power_sum(tiles, peak)

    def step(block, is_even):
        widen(block, even if is_even else odd)
        reduce(block - 1, odd if is_even else even)

    widen(0, even)
    two_by_two(blocks, step)
    reduce(blocks - 1, odd)
    for k in range(cols // LANES):
        lanes = slice(k * LANES, (k + 1) * LANES)
        pot_ref[k : k + 1, :] = merge(peaks[:, lanes], totals[:, lanes])
    repeat(part_ref, pot_ref[...])


def last_kernel(count, parts_ref, sq_ref, out_ref):
    merge_parts(parts_ref, count, out_ref)
    out_ref[...] = out_ref[...] * UNIT + sq_ref[...]


def params():
    return pltpu.CompilerParams(vmem_limit_bytes=VMEM_LIMIT)


def vec(size):
    return jax.ShapeDtypeStruct((size // LANES, LANES), jnp.float32)


def vecs(copies, size):
    return jax.ShapeDtypeStruct((copies, size // LANES, LANES), jnp.float32)


def scratch(*shape):
    return pltpu.VMEM(shape, jnp.float32)


ANYWHERE = pl.BlockSpec(memory_space=pl.ANY)
IN_VMEM = pl.BlockSpec(memory_space=pltpu.VMEM)


def place(own, other, side, side_other, far, theirs, theirs_far, start):
    rows, width = 8 * own.shape[0], own.shape[1]
    return pl.pallas_call(
        place_kernel,
        out_shape=(pltpu.VMEM((rows, width), own.dtype), vec(rows), vec(rows)),
        in_specs=[IN_VMEM] * 8,
        out_specs=(IN_VMEM,) * 3,
        cost_estimate=cost(rows, width, 1),
        compiler_params=params(),
        name="place",
    )(own, other, side, side_other, far, theirs, theirs_far, start)


def bring(*arrays):
    return pl.pallas_call(
        bring_kernel,
        out_shape=tuple(pltpu.VMEM(a.shape, a.dtype) for a in arrays),
        in_specs=[pl.BlockSpec(memory_space=pltpu.HBM)] * len(arrays),
        out_specs=(IN_VMEM,) * len(arrays),
        scratch_shapes=[pltpu.SemaphoreType.DMA] * len(arrays),
        compiler_params=params(),
        name="bring",
    )(*[pltpu.with_memory_space_constraint(a, pltpu.HBM) for a in arrays])


def cost(rows, cols, width):
    return pl.CostEstimate(
        flops=2 * rows * cols * width, bytes_accessed=8 * rows * cols, transcendentals=rows * cols
    )


STEP = 256


def step_scratch():
    return [scratch(LANES, LANES)] * 8


def own_pass(points, targets, pot, rows):
    cols, width = targets.shape
    return pl.pallas_call(
        own_kernel,
        out_shape=(pltpu.VMEM((rows, cols), jnp.float32), vec(rows), vec(rows)),
        in_specs=[IN_VMEM] * 3,
        out_specs=(IN_VMEM,) * 3,
        scratch_shapes=step_scratch(),
        cost_estimate=cost(points.shape[0], cols, width),
        compiler_params=params(),
        name="own_pass",
    )(points, targets, pot)


def more_pass(state, first, second, blocks, targets, pot, copies):
    score, row_parts, src_sq = state
    (rows, cols), width = score.shape, targets.shape[1]
    points = 2 * first.shape[0]
    score = pltpu.with_memory_space_constraint(score, pltpu.VMEM)
    return pl.pallas_call(
        functools.partial(more_kernel, blocks),
        out_shape=(pltpu.VMEM((rows, cols), jnp.float32), vecs(copies, rows), vec(rows)),
        in_specs=[IN_VMEM] * 7,
        out_specs=(IN_VMEM,) * 3,
        scratch_shapes=[scratch(rows // LANES, LANES)] + step_scratch(),
        input_output_aliases={0: 0},
        cost_estimate=cost(points, cols, width),
        compiler_params=params(),
        name="more_pass",
    )(score, row_parts, src_sq, first, second, targets, pot)


def row_pass_call(score, parts, count, copies):
    rows, cols = score.shape
    return pl.pallas_call(
        functools.partial(row_kernel, count),
        out_shape=vecs(copies, rows),
        in_specs=[IN_VMEM] * 2,
        out_specs=IN_VMEM,
        scratch_shapes=[scratch(cols // LANES, LANES), scratch(rows // LANES, LANES)]
        + [scratch(LANES, LANES)] * 4,
        compiler_params=params(),
        name="row_pass",
    )(score, parts)


def col_pass_call(score, parts, sq, count, copies):
    rows, cols = score.shape
    return pl.pallas_call(
        functools.partial(col_kernel, count),
        out_shape=(vec(rows), vecs(copies, cols)),
        in_specs=[IN_VMEM] * 3,
        out_specs=(IN_VMEM, IN_VMEM),
        scratch_shapes=[scratch(max(rows, cols) // LANES, LANES)]
        + [scratch(rows // LANES * SUB, cols)] * 2
        + [scratch(LANES, LANES)] * 2,
        compiler_params=params(),
        name="col_pass",
    )(score, parts, sq)


def last_call(parts, sq, count):
    return pl.pallas_call(
        functools.partial(last_kernel, count),
        out_shape=jax.ShapeDtypeStruct(sq.shape, jnp.float32),
        in_specs=[IN_VMEM] * 2,
        out_specs=IN_VMEM,
        compiler_params=params(),
        name="last",
    )(parts, sq)


def exchange(part, axis):
    return lax.all_to_all(part, axis, 0, 0, tiled=True)


def move(block, to):
    pairs = []
    for z, core, y, x in itertools.product(range(4), range(2), range(4), range(4)):
        a, b, c, d = to(z, core, y, x)
        pairs.append((((z * 2 + core) * 4 + y) * 4 + x, ((a % 4 * 2 + b) * 4 + c % 4) * 4 + d % 4))
    return lax.ppermute(block, ("src", "tgt"), pairs)


def other_core(block):
    return move(block, lambda z, core, y, x: (z, 1 - core, y, x))


def round_z(block):
    return move(block, lambda z, core, y, x: (z + 1 - 2 * core, core, y, x))


def along_line(block, by):
    return move(block, lambda z, core, y, x: (z, core, y + core * by, x + (1 - core) * by))


def across_lines(block, by):
    return move(block, lambda z, core, y, x: (z, core, y + (1 - core) * by, x + core * by))


def after(value, earlier):
    def kernel(*refs):
        del refs

    return pl.pallas_call(
        kernel,
        out_shape=jax.ShapeDtypeStruct(value.shape, value.dtype),
        in_specs=[ANYWHERE] * 2,
        out_specs=ANYWHERE,
        input_output_aliases={0: 0},
        cost_estimate=pl.CostEstimate(flops=0, bytes_accessed=40_000_000, transcendentals=0),
        compiler_params=params(),
        name="after",
    )(value, earlier)


def gather_targets(own, earlier):
    side = round_z(own)
    other = other_core(own)
    far = round_z(after(side, earlier))
    side_other = round_z(other)
    theirs = other_core(jnp.concatenate([side, side_other]))
    return other, side, side_other, far, theirs, other_core(far)


def local(src_points, tgt_points, tgt_start):
    n_src, n_tgt = lax.axis_size("src"), lax.axis_size("tgt")
    own, size = src_points, src_points.shape[0]
    total_src = size * n_tgt * n_src
    total_tgt = tgt_points.shape[0] * n_src * n_tgt
    held, tgt_held, start = bring(own, tgt_points, tgt_start.reshape(-1, LANES))

    line = jnp.concatenate([held, along_line(own, 1), along_line(own, -1), along_line(own, 2)])
    before, behind = across_lines(line, 1), across_lines(line, -1)
    far_low, far_high = across_lines(before[: 2 * size], 1), across_lines(behind[2 * size :], -1)

    targets, tgt_sq, red_g = place(tgt_held, *gather_targets(tgt_points, line), start)
    targets = pltpu.with_memory_space_constraint(targets, pltpu.VMEM)
    state = own_pass(line, targets, red_g, size * n_tgt)
    score, part, src_sq = more_pass(state, before, behind, (12, 4), targets, red_g, 1)
    state = score, part[0], src_sq
    score, part, src_sq = more_pass(state, far_low, far_high, (8, 10), targets, red_g, n_tgt)
    score = pltpu.with_memory_space_constraint(score, pltpu.VMEM)
    for step in range(ITERS):
        if step:
            part = row_pass_call(score, parts, total_src, n_tgt)
        parts = exchange(part, "tgt")
        pot_f, part = col_pass_call(score, parts, src_sq, total_tgt, n_src)
        parts = exchange(part, "src")
    pot_g = last_call(parts, tgt_sq, total_src)
    return (pot_f.reshape(-1), pot_g.reshape(-1))


def solution(mesh):
    return jax.shard_map(
        local,
        mesh=mesh,
        in_specs=(P(("src", "tgt"), None), P(("tgt", "src"), None), P("tgt")),
        out_specs=(P("src"), P("tgt")),
        check_vma=False,
    )
```

```python
import functools
import itertools
import math

import jax
import jax.numpy as jnp
from jax import lax
from jax.experimental import pallas as pl
from jax.experimental.pallas import tpu as pltpu
from jax.sharding import PartitionSpec as P

ITERS = 2


EPSILON = 0.05
UNIT = EPSILON * math.log(2.0)

LANES = 128
SUB = 8
VMEM_LIMIT = 16 * 1024 * 1024


def tree(op, values):
    values = list(values)
    while len(values) > 1:
        values = [
            op(values[i], values[i + 1]) if i + 1 < len(values) else values[i]
            for i in range(0, len(values), 2)
        ]
    return values[0]


def merge(peaks, totals):
    peak = jnp.max(peaks, axis=0, keepdims=True)
    return peak + jnp.log2(jnp.sum(totals * jnp.exp2(peaks - peak), axis=0, keepdims=True))


def merge_parts(parts_ref, count, out_ref):
    parts = [parts_ref[i] for i in range(parts_ref.shape[0])]
    peak = tree(jnp.maximum, parts)
    total = tree(jnp.add, [jnp.exp2(part - peak) for part in parts])
    out_ref[...] = math.log2(count) - (peak + jnp.log2(total))


def repeat(part_ref, part):
    for copy in range(part_ref.shape[0]):
        part_ref[copy] = part


def power_sum(tiles, peak):
    return tree(jnp.add, [jnp.exp2(tile - peak) for tile in tiles])


def lane_tiles(rows):
    return [rows[:, k : k + LANES] for k in range(0, rows.shape[1], LANES)]


def reduce_rows(score_ref, start, groups, pots, peaks, totals):
    for group in groups:
        rows = pl.ds(start + group * SUB, SUB)
        tiles = [tile + pot for tile, pot in zip(lane_tiles(score_ref[rows, :]), pots)]
        peak = tree(jnp.maximum, tiles)
        at = group * SUB
        peaks[at : at + SUB, :] = peak
        totals[at : at + SUB, :] = power_sum(tiles, peak)


def merge_rows(peaks, totals):
    return merge(peaks[...].T, totals[...].T)


def pot_rows(pot_ref):
    return [
        jnp.broadcast_to(pot_ref[k : k + 1, :], (SUB, LANES)) for k in range(pot_ref.shape[0])
    ]


def squares(points):
    wide = points.astype(jnp.float32)
    return jnp.sum(tree(jnp.add, lane_tiles(wide * wide)).T, axis=0, keepdims=True)


def place_kernel(
    own_ref, other_ref, side_ref, side_other_ref, far_ref, theirs_ref, theirs_far_ref, start_ref, targets, sq_ref, pot_ref
):
    own = lax.axis_index("src")
    core = own % 2
    size = own_ref.shape[0]
    chips = targets.shape[0] // (2 * size)

    def put(points, chip, core):
        index = (own // 2 + chip + chips) % chips * 2 + core
        targets[pl.ds(pl.multiple_of(index * size, size), size), :] = points
        per = size // LANES
        for sub in range(per):
            row = squares(points[sub * LANES : (sub + 1) * LANES])
            sq_ref[pl.ds(index * per + sub, 1), :] = row

    side = 2 * core - 1
    put(own_ref[...], 0, core)
    put(other_ref[...], 0, 1 - core)
    put(side_ref[...], side, core)
    put(side_other_ref[...], side, 1 - core)
    put(far_ref[...], 2, core)
    put(theirs_ref[:size, :], -side, 1 - core)
    put(theirs_ref[size:, :], -side, core)
    put(theirs_far_ref[...], 2, 1 - core)
    pot_ref[...] = (start_ref[...] - sq_ref[...]) * (1.0 / UNIT)


def bring_kernel(*refs):
    count = len(refs) // 3
    copies = [
        pltpu.make_async_copy(refs[i], refs[count + i], refs[2 * count + i]) for i in range(count)
    ]
    for copy in copies:
        copy.start()
    for copy in copies:
        copy.wait()


CHUNK = 256


def row_index(block):
    own, core = lax.axis_index("tgt"), lax.axis_index("src") % 2
    y, x = own // 4, own % 4
    line, place = y + core * (x - y), x + core * (y - x)
    at = block % 4
    by = at + 2 * (at % 2) * (1 - at // 2) - at // 2
    to_line, to_place = (line + block // 4) % 4, (place + by) % 4
    return to_line * (4 - 3 * core) + to_place * (1 + 3 * core)


def block_pipeline(sources, tgt_ref, pot_ref, score_ref, rows_ref, sq_ref, peaks, totals):
    per = STEP // LANES
    chunks = tgt_ref.shape[0] // CHUNK
    pots = pot_rows(pot_ref)

    def product(at, chunk):
        ref, first, block = sources[at]
        points = ref[first : first + STEP, :]
        lanes = slice(chunk * CHUNK, (chunk + 1) * CHUNK)
        score_ref[block * LANES : (block + per) * LANES, lanes] = lax.dot_general(
            points, tgt_ref[lanes, :], (((1,), (1,)), ((), ())), preferred_element_type=jnp.float32
        ) * (2.0 / UNIT)
        if chunk < per:
            row = squares(points[chunk * LANES : (chunk + 1) * LANES])
            sq_ref[pl.ds(row_index(block + chunk), 1), :] = row

    def reduce(at, chunk):
        share = chunks // per
        sub, part = chunk // share, chunk % share
        held = at % 2 * per + sub
        start = (sources[at][2] + sub) * LANES
        size = LANES // SUB // share
        groups = range(part * size, (part + 1) * size)
        reduce_rows(score_ref, start, groups, pots, peaks[held], totals[held])

    def finish(at):
        for sub in range(per):
            held = at % 2 * per + sub
            row = merge_rows(peaks[held], totals[held])
            rows_ref[pl.ds(row_index(sources[at][2] + sub), 1), :] = row

    for chunk in range(chunks):
        product(0, chunk)
    for at in range(len(sources)):
        for chunk in range(chunks):
            if at + 1 < len(sources):
                product(at + 1, chunk)
            reduce(at, chunk)
            if at and chunk == chunks // 2:
                finish(at - 1)
    finish(len(sources) - 1)


def own_kernel(points_ref, tgt_ref, pot_ref, score_ref, rows_ref, src_sq_ref, *held):
    sources = [(points_ref, 0, 0), (points_ref, STEP, 2)]
    block_pipeline(sources, tgt_ref, pot_ref, score_ref, rows_ref, src_sq_ref, held[:4], held[4:])


def more_kernel(
    blocks, score_in_ref, rows_in_ref, src_sq_in_ref, tgt_ref, pot_ref, *refs
):
    point_refs, refs = refs[: len(blocks)], refs[len(blocks) :]
    score_ref, part_ref, src_sq_ref, rows_ref, *held = refs
    rows_ref[...] = rows_in_ref[...]
    src_sq_ref[...] = src_sq_in_ref[...]
    sources = [
        (ref, first, block + first // LANES)
        for ref, block in zip(point_refs, blocks)
        for first in range(0, ref.shape[0], STEP)
    ]
    block_pipeline(sources, tgt_ref, pot_ref, score_ref, rows_ref, src_sq_ref, held[:4], held[4:])
    repeat(part_ref, rows_ref[...])


def two_by_two(blocks, step):
    step(1, False)

    @pl.loop(1, blocks // 2)
    def _(pair):
        step(2 * pair, True)
        step(2 * pair + 1, False)


def row_kernel(count, score_ref, parts_ref, part_ref, pot_ref, rows_ref, *held):
    merge_parts(parts_ref, count, pot_ref)
    pots = pot_rows(pot_ref)
    blocks = score_ref.shape[0] // LANES
    even, odd = held[:2], held[2:]

    def reduce(block, into):
        start = pl.multiple_of(block * LANES, LANES)
        reduce_rows(score_ref, start, range(LANES // SUB), pots, *into)

    def finish(block, held):
        rows_ref[pl.ds(row_index(block), 1), :] = merge_rows(*held)

    def step(block, is_even):
        finish(block - 1, odd if is_even else even)
        reduce(block, even if is_even else odd)

    reduce(0, even)
    two_by_two(blocks, step)
    finish(blocks - 1, odd)
    repeat(part_ref, rows_ref[...])


def col_kernel(
    count, score_ref, parts_ref, pot_ref, part_ref, peaks, totals, even, odd
):
    merge_parts(parts_ref, count, pot_ref)
    rows, cols = score_ref.shape
    blocks = rows // LANES

    def widen(block, into):
        row = pot_ref[pl.ds(row_index(block), 1), :]
        into[...] = jnp.broadcast_to(row, (LANES, LANES)).T

    def reduce(block, wide):
        here = pl.ds(pl.multiple_of(block * LANES, LANES), LANES)
        there = pl.ds(pl.multiple_of(block * SUB, SUB), SUB)
        pots = wide[...]
        for k in range(cols // LANES):
            lanes = slice(k * LANES, (k + 1) * LANES)
            tile = score_ref[here, lanes] + pots
            tiles = [tile[i : i + SUB] for i in range(0, LANES, SUB)]
            peak = tree(jnp.maximum, tiles)
            peaks[there, lanes] = peak
            totals[there, lanes] = power_sum(tiles, peak)

    def step(block, is_even):
        widen(block, even if is_even else odd)
        reduce(block - 1, odd if is_even else even)

    widen(0, even)
    two_by_two(blocks, step)
    reduce(blocks - 1, odd)
    for k in range(cols // LANES):
        lanes = slice(k * LANES, (k + 1) * LANES)
        part_ref[0, k : k + 1, :] = merge(peaks[:, lanes], totals[:, lanes])
    repeat(part_ref, part_ref[0])


def last_kernel(count, parts_ref, pot_f_ref, src_sq_ref, tgt_sq_ref, out_f_ref, out_g_ref):
    out_f_ref[...] = pot_f_ref[...] * UNIT + src_sq_ref[...]
    merge_parts(parts_ref, count, out_g_ref)
    out_g_ref[...] = out_g_ref[...] * UNIT + tgt_sq_ref[...]


def params():
    return pltpu.CompilerParams(vmem_limit_bytes=VMEM_LIMIT)


def vec(size):
    return jax.ShapeDtypeStruct((size // LANES, LANES), jnp.float32)


def vecs(copies, size):
    return jax.ShapeDtypeStruct((copies, size // LANES, LANES), jnp.float32)


def scratch(*shape):
    return pltpu.VMEM(shape, jnp.float32)


ANYWHERE = pl.BlockSpec(memory_space=pl.ANY)
IN_VMEM = pl.BlockSpec(memory_space=pltpu.VMEM)


def place(own, other, side, side_other, far, theirs, theirs_far, start):
    rows, width = 8 * own.shape[0], own.shape[1]
    return pl.pallas_call(
        place_kernel,
        out_shape=(pltpu.VMEM((rows, width), own.dtype), vec(rows), vec(rows)),
        in_specs=[IN_VMEM] * 8,
        out_specs=(IN_VMEM,) * 3,
        cost_estimate=cost(rows, width, 1),
        compiler_params=params(),
        name="place",
    )(own, other, side, side_other, far, theirs, theirs_far, start)


def bring(*arrays):
    return pl.pallas_call(
        bring_kernel,
        out_shape=tuple(pltpu.VMEM(a.shape, a.dtype) for a in arrays),
        in_specs=[pl.BlockSpec(memory_space=pltpu.HBM)] * len(arrays),
        out_specs=(IN_VMEM,) * len(arrays),
        scratch_shapes=[pltpu.SemaphoreType.DMA] * len(arrays),
        compiler_params=params(),
        name="bring",
    )(*[pltpu.with_memory_space_constraint(a, pltpu.HBM) for a in arrays])


def cost(rows, cols, width):
    return pl.CostEstimate(
        flops=2 * rows * cols * width, bytes_accessed=8 * rows * cols, transcendentals=rows * cols
    )


STEP = 256


def step_scratch():
    return [scratch(LANES, LANES)] * 8


def own_pass(points, targets, pot, rows):
    cols, width = targets.shape
    return pl.pallas_call(
        own_kernel,
        out_shape=(pltpu.VMEM((rows, cols), jnp.float32), vec(rows), vec(rows)),
        in_specs=[IN_VMEM] * 3,
        out_specs=(IN_VMEM,) * 3,
        scratch_shapes=step_scratch(),
        cost_estimate=cost(points.shape[0], cols, width),
        compiler_params=params(),
        name="own_pass",
    )(points, targets, pot)


def more_pass(state, points, blocks, targets, pot, copies):
    score, row_parts, src_sq = state
    (rows, cols), width = score.shape, targets.shape[1]
    added = sum(array.shape[0] for array in points)
    score = pltpu.with_memory_space_constraint(score, pltpu.VMEM)
    return pl.pallas_call(
        functools.partial(more_kernel, blocks),
        out_shape=(pltpu.VMEM((rows, cols), jnp.float32), vecs(copies, rows), vec(rows)),
        in_specs=[IN_VMEM] * (5 + len(points)),
        out_specs=(IN_VMEM,) * 3,
        scratch_shapes=[scratch(rows // LANES, LANES)] + step_scratch(),
        input_output_aliases={0: 0},
        cost_estimate=cost(added, cols, width),
        compiler_params=params(),
        name="more_pass",
    )(score, row_parts, src_sq, targets, pot, *points)


def row_pass_call(score, parts, count, copies):
    rows, cols = score.shape
    return pl.pallas_call(
        functools.partial(row_kernel, count),
        out_shape=vecs(copies, rows),
        in_specs=[IN_VMEM] * 2,
        out_specs=IN_VMEM,
        scratch_shapes=[scratch(cols // LANES, LANES), scratch(rows // LANES, LANES)]
        + [scratch(LANES, LANES)] * 4,
        compiler_params=params(),
        name="row_pass",
    )(score, parts)


def col_pass_call(score, parts, count, copies):
    rows, cols = score.shape
    return pl.pallas_call(
        functools.partial(col_kernel, count),
        out_shape=(pltpu.VMEM((rows // LANES, LANES), jnp.float32), vecs(copies, cols)),
        in_specs=[IN_VMEM] * 2,
        out_specs=(IN_VMEM, IN_VMEM),
        scratch_shapes=[scratch(rows // LANES * SUB, cols)] * 2 + [scratch(LANES, LANES)] * 2,
        compiler_params=params(),
        name="col_pass",
    )(score, parts)


def last_call(parts, pot_f, src_sq, tgt_sq, count):
    return pl.pallas_call(
        functools.partial(last_kernel, count),
        out_shape=(vec(src_sq.size), vec(tgt_sq.size)),
        in_specs=[IN_VMEM] * 4,
        out_specs=(IN_VMEM, IN_VMEM),
        compiler_params=params(),
        name="last",
    )(parts, pltpu.with_memory_space_constraint(pot_f, pltpu.VMEM), src_sq, tgt_sq)


def exchange(part, axis):
    return lax.all_to_all(part, axis, 0, 0, tiled=True)


def move(block, to):
    pairs = []
    for z, core, y, x in itertools.product(range(4), range(2), range(4), range(4)):
        a, b, c, d = to(z, core, y, x)
        pairs.append((((z * 2 + core) * 4 + y) * 4 + x, ((a % 4 * 2 + b) * 4 + c % 4) * 4 + d % 4))
    return lax.ppermute(block, ("src", "tgt"), pairs)


def other_core(block):
    return move(block, lambda z, core, y, x: (z, 1 - core, y, x))


def round_z(block):
    return move(block, lambda z, core, y, x: (z + 1 - 2 * core, core, y, x))


def along_line(block, by):
    return move(block, lambda z, core, y, x: (z, core, y + core * by, x + (1 - core) * by))


def across_lines(block, by):
    return move(block, lambda z, core, y, x: (z, core, y + (1 - core) * by, x + core * by))


def after(value, earlier):
    def kernel(*refs):
        del refs

    return pl.pallas_call(
        kernel,
        out_shape=jax.ShapeDtypeStruct(value.shape, value.dtype),
        in_specs=[ANYWHERE] * 2,
        out_specs=ANYWHERE,
        input_output_aliases={0: 0},
        cost_estimate=pl.CostEstimate(flops=0, bytes_accessed=40_000_000, transcendentals=0),
        compiler_params=params(),
        name="after",
    )(value, earlier)


def gather_targets(own, earlier):
    side = round_z(own)
    other = other_core(own)
    far = round_z(after(side, earlier))
    side_other = round_z(other)
    theirs = other_core(jnp.concatenate([side, side_other]))
    return other, side, side_other, far, theirs, other_core(far)


def local(src_points, tgt_points, tgt_start):
    n_src, n_tgt = lax.axis_size("src"), lax.axis_size("tgt")
    own, size = src_points, src_points.shape[0]
    total_src = size * n_tgt * n_src
    total_tgt = tgt_points.shape[0] * n_src * n_tgt
    held, tgt_held, start = bring(own, tgt_points, tgt_start.reshape(-1, LANES))

    line = jnp.concatenate([held, along_line(own, 1), along_line(own, -1), along_line(own, 2)])
    before, behind = across_lines(line, 1), across_lines(line, -1)
    far = across_lines(before, 1)

    targets, tgt_sq, red_g = place(tgt_held, *gather_targets(tgt_points, line), start)
    targets = pltpu.with_memory_space_constraint(targets, pltpu.VMEM)
    state = own_pass(line, targets, red_g, size * n_tgt)
    score, part, src_sq = more_pass(state, (before, behind), (12, 4), targets, red_g, 1)
    state = score, part[0], src_sq
    score, part, src_sq = more_pass(state, (far,), (8,), targets, red_g, n_tgt)
    score = pltpu.with_memory_space_constraint(score, pltpu.VMEM)
    for step in range(ITERS):
        if step:
            part = row_pass_call(score, parts, total_src, n_tgt)
        parts = exchange(part, "tgt")
        red_f, part = col_pass_call(score, parts, total_tgt, n_src)
        parts = exchange(part, "src")
    pot_f, pot_g = last_call(parts, red_f, src_sq, tgt_sq, total_src)
    return (pot_f.reshape(-1), pot_g.reshape(-1))


def solution(mesh):
    return jax.shard_map(
        local,
        mesh=mesh,
        in_specs=(P(("src", "tgt"), None), P(("tgt", "src"), None), P("tgt")),
        out_specs=(P("src"), P("tgt")),
        check_vma=False,
    )
```

```python
import functools
import itertools
import math

import jax
import jax.numpy as jnp
from jax import lax
from jax.experimental import pallas as pl
from jax.experimental.pallas import tpu as pltpu
from jax.sharding import PartitionSpec as P

ITERS = 2


EPSILON = 0.05
UNIT = EPSILON * math.log(2.0)

LANES = 128
SUB = 8
VMEM_LIMIT = 16 * 1024 * 1024


def tree(op, values):
    values = list(values)
    while len(values) > 1:
        values = [
            op(values[i], values[i + 1]) if i + 1 < len(values) else values[i]
            for i in range(0, len(values), 2)
        ]
    return values[0]


def merge(peaks, totals):
    peak = jnp.max(peaks, axis=0, keepdims=True)
    return peak + jnp.log2(jnp.sum(totals * jnp.exp2(peaks - peak), axis=0, keepdims=True))


def merge_parts(parts_ref, count, out_ref):
    parts = [parts_ref[i] for i in range(parts_ref.shape[0])]
    peak = tree(jnp.maximum, parts)
    total = tree(jnp.add, [jnp.exp2(part - peak) for part in parts])
    out_ref[...] = math.log2(count) - (peak + jnp.log2(total))


def repeat(part_ref, part):
    for copy in range(part_ref.shape[0]):
        part_ref[copy] = part


def power_sum(tiles, peak):
    return tree(jnp.add, [jnp.exp2(tile - peak) for tile in tiles])


def lane_tiles(rows):
    return [rows[:, k : k + LANES] for k in range(0, rows.shape[1], LANES)]


def reduce_rows(score_ref, start, groups, pots, peaks, totals):
    for group in groups:
        rows = pl.ds(start + group * SUB, SUB)
        tiles = [tile + pot for tile, pot in zip(lane_tiles(score_ref[rows, :]), pots)]
        peak = tree(jnp.maximum, tiles)
        at = group * SUB
        peaks[at : at + SUB, :] = peak
        totals[at : at + SUB, :] = power_sum(tiles, peak)


def merge_rows(peaks, totals):
    return merge(peaks[...].T, totals[...].T)


def pot_rows(pot_ref):
    return [
        jnp.broadcast_to(pot_ref[k : k + 1, :], (SUB, LANES)) for k in range(pot_ref.shape[0])
    ]


def squares(points):
    wide = points.astype(jnp.float32)
    return jnp.sum(tree(jnp.add, lane_tiles(wide * wide)).T, axis=0, keepdims=True)


def place_kernel(
    own_ref, other_ref, side_ref, side_other_ref, far_ref, theirs_ref, theirs_far_ref, start_ref, targets, sq_ref, pot_ref
):
    own = lax.axis_index("src")
    core = own % 2
    size = own_ref.shape[0]
    chips = targets.shape[0] // (2 * size)

    def put(points, chip, core):
        index = (own // 2 + chip + chips) % chips * 2 + core
        targets[pl.ds(pl.multiple_of(index * size, size), size), :] = points
        per = size // LANES
        for sub in range(per):
            row = squares(points[sub * LANES : (sub + 1) * LANES])
            sq_ref[pl.ds(index * per + sub, 1), :] = row

    side = 2 * core - 1
    put(own_ref[...], 0, core)
    put(other_ref[...], 0, 1 - core)
    put(side_ref[...], side, core)
    put(side_other_ref[...], side, 1 - core)
    put(far_ref[...], 2, core)
    put(theirs_ref[:size, :], -side, 1 - core)
    put(theirs_ref[size:, :], -side, core)
    put(theirs_far_ref[...], 2, 1 - core)
    pot_ref[...] = (start_ref[...] - sq_ref[...]) * (1.0 / UNIT)


def bring_kernel(*refs):
    count = len(refs) // 3
    copies = [
        pltpu.make_async_copy(refs[i], refs[count + i], refs[2 * count + i]) for i in range(count)
    ]
    for copy in copies:
        copy.start()
    for copy in copies:
        copy.wait()


CHUNK = 256


def row_index(block):
    own, core = lax.axis_index("tgt"), lax.axis_index("src") % 2
    y, x = own // 4, own % 4
    line, place = y + core * (x - y), x + core * (y - x)
    at = block % 4
    by = at + (at + 3) // 4 + at // 3
    to_line, to_place = (line + block // 4) % 4, (place + by) % 4
    return to_line * (4 - 3 * core) + to_place * (1 + 3 * core)


def block_pipeline(sources, tgt_ref, pot_ref, score_ref, rows_ref, sq_ref, peaks, totals):
    per = STEP // LANES
    chunks = tgt_ref.shape[0] // CHUNK
    pots = pot_rows(pot_ref)

    def product(at, chunk):
        ref, first, block = sources[at]
        points = ref[first : first + STEP, :]
        lanes = slice(chunk * CHUNK, (chunk + 1) * CHUNK)
        score_ref[block * LANES : (block + per) * LANES, lanes] = lax.dot_general(
            points, tgt_ref[lanes, :], (((1,), (1,)), ((), ())), preferred_element_type=jnp.float32
        ) * (2.0 / UNIT)
        if chunk < per:
            row = squares(points[chunk * LANES : (chunk + 1) * LANES])
            sq_ref[pl.ds(row_index(block + chunk), 1), :] = row

    def reduce(at, chunk):
        share = chunks // per
        sub, part = chunk // share, chunk % share
        held = at % 2 * per + sub
        start = (sources[at][2] + sub) * LANES
        size = LANES // SUB // share
        groups = range(part * size, (part + 1) * size)
        reduce_rows(score_ref, start, groups, pots, peaks[held], totals[held])

    def finish(at):
        for sub in range(per):
            held = at % 2 * per + sub
            row = merge_rows(peaks[held], totals[held])
            rows_ref[pl.ds(row_index(sources[at][2] + sub), 1), :] = row

    for chunk in range(chunks):
        product(0, chunk)
    for at in range(len(sources)):
        for chunk in range(chunks):
            if at + 1 < len(sources):
                product(at + 1, chunk)
            reduce(at, chunk)
            if at and chunk == chunks // 2:
                finish(at - 1)
    finish(len(sources) - 1)


def own_kernel(points_ref, tgt_ref, pot_ref, score_ref, rows_ref, src_sq_ref, *held):
    sources = [(points_ref, 0, 0), (points_ref, STEP, 2)]
    block_pipeline(sources, tgt_ref, pot_ref, score_ref, rows_ref, src_sq_ref, held[:4], held[4:])


def more_kernel(
    blocks, score_in_ref, rows_in_ref, src_sq_in_ref, tgt_ref, pot_ref, *refs
):
    point_refs, refs = refs[: len(blocks)], refs[len(blocks) :]
    score_ref, part_ref, src_sq_ref, rows_ref, *held = refs
    rows_ref[...] = rows_in_ref[...]
    src_sq_ref[...] = src_sq_in_ref[...]
    sources = [
        (ref, first, block + first // LANES)
        for ref, block in zip(point_refs, blocks)
        for first in range(0, ref.shape[0], STEP)
    ]
    block_pipeline(sources, tgt_ref, pot_ref, score_ref, rows_ref, src_sq_ref, held[:4], held[4:])
    repeat(part_ref, rows_ref[...])


def two_by_two(blocks, step):
    step(1, False)

    @pl.loop(1, blocks // 2)
    def _(pair):
        step(2 * pair, True)
        step(2 * pair + 1, False)


def row_kernel(count, score_ref, parts_ref, part_ref, pot_ref, rows_ref, *held):
    merge_parts(parts_ref, count, pot_ref)
    pots = pot_rows(pot_ref)
    blocks = score_ref.shape[0] // LANES
    even, odd = held[:2], held[2:]

    def reduce(block, into):
        start = pl.multiple_of(block * LANES, LANES)
        reduce_rows(score_ref, start, range(LANES // SUB), pots, *into)

    def finish(block, held):
        rows_ref[pl.ds(row_index(block), 1), :] = merge_rows(*held)

    def step(block, is_even):
        finish(block - 1, odd if is_even else even)
        reduce(block, even if is_even else odd)

    reduce(0, even)
    two_by_two(blocks, step)
    finish(blocks - 1, odd)
    repeat(part_ref, rows_ref[...])


def col_kernel(
    count, score_ref, parts_ref, pot_ref, part_ref, peaks, totals, even, odd
):
    merge_parts(parts_ref, count, pot_ref)
    rows, cols = score_ref.shape
    blocks = rows // LANES

    def widen(block, into):
        row = pot_ref[pl.ds(row_index(block), 1), :]
        into[...] = jnp.broadcast_to(row, (LANES, LANES)).T

    def reduce(block, wide):
        here = pl.ds(pl.multiple_of(block * LANES, LANES), LANES)
        there = pl.ds(pl.multiple_of(block * SUB, SUB), SUB)
        pots = wide[...]
        for k in range(cols // LANES):
            lanes = slice(k * LANES, (k + 1) * LANES)
            tile = score_ref[here, lanes] + pots
            tiles = [tile[i : i + SUB] for i in range(0, LANES, SUB)]
            peak = tree(jnp.maximum, tiles)
            peaks[there, lanes] = peak
            totals[there, lanes] = power_sum(tiles, peak)

    def step(block, is_even):
        widen(block, even if is_even else odd)
        reduce(block - 1, odd if is_even else even)

    widen(0, even)
    two_by_two(blocks, step)
    reduce(blocks - 1, odd)
    for k in range(cols // LANES):
        lanes = slice(k * LANES, (k + 1) * LANES)
        part_ref[0, k : k + 1, :] = merge(peaks[:, lanes], totals[:, lanes])
    repeat(part_ref, part_ref[0])


def last_kernel(count, parts_ref, pot_f_ref, src_sq_ref, tgt_sq_ref, out_f_ref, out_g_ref):
    out_f_ref[...] = pot_f_ref[...] * UNIT + src_sq_ref[...]
    merge_parts(parts_ref, count, out_g_ref)
    out_g_ref[...] = out_g_ref[...] * UNIT + tgt_sq_ref[...]


def params():
    return pltpu.CompilerParams(vmem_limit_bytes=VMEM_LIMIT)


def vec(size):
    return jax.ShapeDtypeStruct((size // LANES, LANES), jnp.float32)


def vecs(copies, size):
    return jax.ShapeDtypeStruct((copies, size // LANES, LANES), jnp.float32)


def scratch(*shape):
    return pltpu.VMEM(shape, jnp.float32)


ANYWHERE = pl.BlockSpec(memory_space=pl.ANY)
IN_VMEM = pl.BlockSpec(memory_space=pltpu.VMEM)


def place(own, other, side, side_other, far, theirs, theirs_far, start):
    rows, width = 8 * own.shape[0], own.shape[1]
    return pl.pallas_call(
        place_kernel,
        out_shape=(pltpu.VMEM((rows, width), own.dtype), vec(rows), vec(rows)),
        in_specs=[IN_VMEM] * 8,
        out_specs=(IN_VMEM,) * 3,
        cost_estimate=cost(rows, width, 1),
        compiler_params=params(),
        name="place",
    )(own, other, side, side_other, far, theirs, theirs_far, start)


def bring(*arrays):
    return pl.pallas_call(
        bring_kernel,
        out_shape=tuple(pltpu.VMEM(a.shape, a.dtype) for a in arrays),
        in_specs=[pl.BlockSpec(memory_space=pltpu.HBM)] * len(arrays),
        out_specs=(IN_VMEM,) * len(arrays),
        scratch_shapes=[pltpu.SemaphoreType.DMA] * len(arrays),
        compiler_params=params(),
        name="bring",
    )(*[pltpu.with_memory_space_constraint(a, pltpu.HBM) for a in arrays])


def cost(rows, cols, width):
    return pl.CostEstimate(
        flops=2 * rows * cols * width, bytes_accessed=8 * rows * cols, transcendentals=rows * cols
    )


STEP = 256


def step_scratch():
    return [scratch(LANES, LANES)] * 8


def own_pass(points, targets, pot, rows):
    cols, width = targets.shape
    return pl.pallas_call(
        own_kernel,
        out_shape=(pltpu.VMEM((rows, cols), jnp.float32), vec(rows), vec(rows)),
        in_specs=[IN_VMEM] * 3,
        out_specs=(IN_VMEM,) * 3,
        scratch_shapes=step_scratch(),
        cost_estimate=cost(points.shape[0], cols, width),
        compiler_params=params(),
        name="own_pass",
    )(points, targets, pot)


def more_pass(state, points, blocks, targets, pot, copies):
    score, row_parts, src_sq = state
    (rows, cols), width = score.shape, targets.shape[1]
    added = sum(array.shape[0] for array in points)
    score = pltpu.with_memory_space_constraint(score, pltpu.VMEM)
    return pl.pallas_call(
        functools.partial(more_kernel, blocks),
        out_shape=(pltpu.VMEM((rows, cols), jnp.float32), vecs(copies, rows), vec(rows)),
        in_specs=[IN_VMEM] * (5 + len(points)),
        out_specs=(IN_VMEM,) * 3,
        scratch_shapes=[scratch(rows // LANES, LANES)] + step_scratch(),
        input_output_aliases={0: 0},
        cost_estimate=cost(added, cols, width),
        compiler_params=params(),
        name="more_pass",
    )(score, row_parts, src_sq, targets, pot, *points)


def row_pass_call(score, parts, count, copies):
    rows, cols = score.shape
    return pl.pallas_call(
        functools.partial(row_kernel, count),
        out_shape=vecs(copies, rows),
        in_specs=[IN_VMEM] * 2,
        out_specs=IN_VMEM,
        scratch_shapes=[scratch(cols // LANES, LANES), scratch(rows // LANES, LANES)]
        + [scratch(LANES, LANES)] * 4,
        compiler_params=params(),
        name="row_pass",
    )(score, parts)


def col_pass_call(score, parts, count, copies):
    rows, cols = score.shape
    return pl.pallas_call(
        functools.partial(col_kernel, count),
        out_shape=(pltpu.VMEM((rows // LANES, LANES), jnp.float32), vecs(copies, cols)),
        in_specs=[IN_VMEM] * 2,
        out_specs=(IN_VMEM, IN_VMEM),
        scratch_shapes=[scratch(rows // LANES * SUB, cols)] * 2 + [scratch(LANES, LANES)] * 2,
        compiler_params=params(),
        name="col_pass",
    )(score, parts)


def last_call(parts, pot_f, src_sq, tgt_sq, count):
    return pl.pallas_call(
        functools.partial(last_kernel, count),
        out_shape=(vec(src_sq.size), vec(tgt_sq.size)),
        in_specs=[IN_VMEM] * 4,
        out_specs=(IN_VMEM, IN_VMEM),
        compiler_params=params(),
        name="last",
    )(parts, pltpu.with_memory_space_constraint(pot_f, pltpu.VMEM), src_sq, tgt_sq)


def exchange(part, axis):
    return lax.all_to_all(part, axis, 0, 0, tiled=True)


def move(block, to):
    pairs = []
    for z, core, y, x in itertools.product(range(4), range(2), range(4), range(4)):
        a, b, c, d = to(z, core, y, x)
        pairs.append((((z * 2 + core) * 4 + y) * 4 + x, ((a % 4 * 2 + b) * 4 + c % 4) * 4 + d % 4))
    return lax.ppermute(block, ("src", "tgt"), pairs)


def other_core(block):
    return move(block, lambda z, core, y, x: (z, 1 - core, y, x))


def round_z(block):
    return move(block, lambda z, core, y, x: (z + 1 - 2 * core, core, y, x))


def along_line(block, by):
    return move(block, lambda z, core, y, x: (z, core, y + core * by, x + (1 - core) * by))


def across_lines(block, by):
    return move(block, lambda z, core, y, x: (z, core, y + (1 - core) * by, x + core * by))


def after(value, earlier):
    def kernel(*refs):
        del refs

    return pl.pallas_call(
        kernel,
        out_shape=jax.ShapeDtypeStruct(value.shape, value.dtype),
        in_specs=[ANYWHERE] * 2,
        out_specs=ANYWHERE,
        input_output_aliases={0: 0},
        cost_estimate=pl.CostEstimate(flops=0, bytes_accessed=40_000_000, transcendentals=0),
        compiler_params=params(),
        name="after",
    )(value, earlier)


def gather_targets(own, earlier):
    side = round_z(own)
    other = other_core(own)
    far = round_z(after(side, earlier))
    side_other = round_z(other)
    theirs = other_core(jnp.concatenate([side, side_other]))
    return other, side, side_other, far, theirs, other_core(far)


def local(src_points, tgt_points, tgt_start):
    n_src, n_tgt = lax.axis_size("src"), lax.axis_size("tgt")
    own, size = src_points, src_points.shape[0]
    total_src = size * n_tgt * n_src
    total_tgt = tgt_points.shape[0] * n_src * n_tgt
    held, tgt_held, start = bring(own, tgt_points, tgt_start.reshape(-1, LANES))

    line = jnp.concatenate([held, along_line(own, 2), along_line(own, 1), along_line(own, -1)])
    before, behind = across_lines(line, 1), across_lines(line, -1)
    far = across_lines(before, 1)

    targets, tgt_sq, red_g = place(tgt_held, *gather_targets(tgt_points, line), start)
    targets = pltpu.with_memory_space_constraint(targets, pltpu.VMEM)
    state = own_pass(line, targets, red_g, size * n_tgt)
    for points, block in ((before, 12), (behind, 4)):
        score, part, src_sq = more_pass(state, (points,), (block,), targets, red_g, 1)
        state = score, part[0], src_sq
    score, part, src_sq = more_pass(state, (far,), (8,), targets, red_g, n_tgt)
    score = pltpu.with_memory_space_constraint(score, pltpu.VMEM)
    for step in range(ITERS):
        if step:
            part = row_pass_call(score, parts, total_src, n_tgt)
        parts = exchange(part, "tgt")
        red_f, part = col_pass_call(score, parts, total_tgt, n_src)
        parts = exchange(part, "src")
    pot_f, pot_g = last_call(parts, red_f, src_sq, tgt_sq, total_src)
    return (pot_f.reshape(-1), pot_g.reshape(-1))


def solution(mesh):
    return jax.shard_map(
        local,
        mesh=mesh,
        in_specs=(P(("src", "tgt"), None), P(("tgt", "src"), None), P("tgt")),
        out_specs=(P("src"), P("tgt")),
        check_vma=False,
    )
```

```python
import functools
import itertools
import math

import jax
import jax.numpy as jnp
from jax import lax
from jax.experimental import pallas as pl
from jax.experimental.pallas import tpu as pltpu
from jax.sharding import PartitionSpec as P

ITERS = 2


EPSILON = 0.05
UNIT = EPSILON * math.log(2.0)

LANES = 128
SUB = 8
VMEM_LIMIT = 16 * 1024 * 1024


def tree(op, values):
    values = list(values)
    while len(values) > 1:
        values = [
            op(values[i], values[i + 1]) if i + 1 < len(values) else values[i]
            for i in range(0, len(values), 2)
        ]
    return values[0]


def merge(peaks, totals):
    peak = jnp.max(peaks, axis=0, keepdims=True)
    return peak + jnp.log2(jnp.sum(totals * jnp.exp2(peaks - peak), axis=0, keepdims=True))


def merge_parts(parts_ref, count, out_ref):
    parts = [parts_ref[i] for i in range(parts_ref.shape[0])]
    peak = tree(jnp.maximum, parts)
    total = tree(jnp.add, [jnp.exp2(part - peak) for part in parts])
    out_ref[...] = math.log2(count) - (peak + jnp.log2(total))


def repeat(part_ref, part):
    for copy in range(part_ref.shape[0]):
        part_ref[copy] = part


def power_sum(tiles, peak):
    return tree(jnp.add, [jnp.exp2(tile - peak) for tile in tiles])


def lane_tiles(rows):
    return [rows[:, k : k + LANES] for k in range(0, rows.shape[1], LANES)]


def reduce_rows(score_ref, start, groups, pots, peaks, totals):
    for group in groups:
        rows = pl.ds(start + group * SUB, SUB)
        tiles = [tile + pot for tile, pot in zip(lane_tiles(score_ref[rows, :]), pots)]
        peak = tree(jnp.maximum, tiles)
        at = group * SUB
        peaks[at : at + SUB, :] = peak
        totals[at : at + SUB, :] = power_sum(tiles, peak)


def merge_rows(peaks, totals):
    return merge(peaks[...].T, totals[...].T)


def pot_rows(pot_ref):
    return [
        jnp.broadcast_to(pot_ref[k : k + 1, :], (SUB, LANES)) for k in range(pot_ref.shape[0])
    ]


def squares(points):
    wide = points.astype(jnp.float32)
    return jnp.sum(tree(jnp.add, lane_tiles(wide * wide)).T, axis=0, keepdims=True)


def place_kernel(
    own_ref, other_ref, side_ref, side_other_ref, far_ref, theirs_ref, theirs_far_ref, start_ref, targets, sq_ref, pot_ref
):
    own = lax.axis_index("src")
    core = own % 2
    size = own_ref.shape[0]
    chips = targets.shape[1] // (2 * size)

    def put(points, chip, core):
        index = (own // 2 + chip + chips) % chips * 2 + core
        targets[:, pl.ds(pl.multiple_of(index * size, size), size)] = points.T
        per = size // LANES
        for sub in range(per):
            row = squares(points[sub * LANES : (sub + 1) * LANES])
            sq_ref[pl.ds(index * per + sub, 1), :] = row

    side = 2 * core - 1
    put(own_ref[...], 0, core)
    put(other_ref[...], 0, 1 - core)
    put(side_ref[...], side, core)
    put(side_other_ref[...], side, 1 - core)
    put(far_ref[...], 2, core)
    put(theirs_ref[:size, :], -side, 1 - core)
    put(theirs_ref[size:, :], -side, core)
    put(theirs_far_ref[...], 2, 1 - core)
    pot_ref[...] = (start_ref[...] - sq_ref[...]) * (1.0 / UNIT)


def bring_kernel(*refs):
    count = len(refs) // 3
    copies = [
        pltpu.make_async_copy(refs[i], refs[count + i], refs[2 * count + i]) for i in range(count)
    ]
    for copy in copies:
        copy.start()
    for copy in copies:
        copy.wait()


CHUNK = 256


def row_index(block):
    own, core = lax.axis_index("tgt"), lax.axis_index("src") % 2
    y, x = own // 4, own % 4
    line, place = y + core * (x - y), x + core * (y - x)
    at = block % 4
    by = at + (at + 3) // 4 + at // 3
    to_line, to_place = (line + block // 4) % 4, (place + by) % 4
    return to_line * (4 - 3 * core) + to_place * (1 + 3 * core)


def block_pipeline(sources, tgt_ref, pot_ref, score_ref, rows_ref, sq_ref, peaks, totals):
    per = STEP // LANES
    chunks = tgt_ref.shape[1] // CHUNK
    pots = pot_rows(pot_ref)

    def product(at, chunk):
        ref, first, block = sources[at]
        points = ref[first : first + STEP, :]
        lanes = slice(chunk * CHUNK, (chunk + 1) * CHUNK)
        score_ref[block * LANES : (block + per) * LANES, lanes] = lax.dot_general(
            points, tgt_ref[:, lanes], (((1,), (0,)), ((), ())), preferred_element_type=jnp.float32
        ) * (2.0 / UNIT)
        if chunk < per:
            row = squares(points[chunk * LANES : (chunk + 1) * LANES])
            sq_ref[pl.ds(row_index(block + chunk), 1), :] = row

    def reduce(at, chunk):
        share = chunks // per
        sub, part = chunk // share, chunk % share
        held = at % 2 * per + sub
        start = (sources[at][2] + sub) * LANES
        size = LANES // SUB // share
        groups = range(part * size, (part + 1) * size)
        reduce_rows(score_ref, start, groups, pots, peaks[held], totals[held])

    def finish(at):
        for sub in range(per):
            held = at % 2 * per + sub
            row = merge_rows(peaks[held], totals[held])
            rows_ref[pl.ds(row_index(sources[at][2] + sub), 1), :] = row

    for chunk in range(chunks):
        product(0, chunk)
    for at in range(len(sources)):
        for chunk in range(chunks):
            if at + 1 < len(sources):
                product(at + 1, chunk)
            reduce(at, chunk)
            if at and chunk == chunks // 2:
                finish(at - 1)
    finish(len(sources) - 1)


def own_kernel(points_ref, tgt_ref, pot_ref, score_ref, rows_ref, src_sq_ref, *held):
    sources = [(points_ref, 0, 0), (points_ref, STEP, 2)]
    block_pipeline(sources, tgt_ref, pot_ref, score_ref, rows_ref, src_sq_ref, held[:4], held[4:])


def more_kernel(
    blocks, score_in_ref, rows_in_ref, src_sq_in_ref, tgt_ref, pot_ref, *refs
):
    point_refs, refs = refs[: len(blocks)], refs[len(blocks) :]
    score_ref, part_ref, src_sq_ref, rows_ref, *held = refs
    rows_ref[...] = rows_in_ref[...]
    src_sq_ref[...] = src_sq_in_ref[...]
    sources = [
        (ref, first, block + first // LANES)
        for ref, block in zip(point_refs, blocks)
        for first in range(0, ref.shape[0], STEP)
    ]
    block_pipeline(sources, tgt_ref, pot_ref, score_ref, rows_ref, src_sq_ref, held[:4], held[4:])
    repeat(part_ref, rows_ref[...])


def two_by_two(blocks, step):
    step(1, False)

    @pl.loop(1, blocks // 2)
    def _(pair):
        step(2 * pair, True)
        step(2 * pair + 1, False)


def row_kernel(count, score_ref, parts_ref, part_ref, pot_ref, rows_ref, *held):
    merge_parts(parts_ref, count, pot_ref)
    pots = pot_rows(pot_ref)
    blocks = score_ref.shape[0] // LANES
    even, odd = held[:2], held[2:]

    def reduce(block, into):
        start = pl.multiple_of(block * LANES, LANES)
        reduce_rows(score_ref, start, range(LANES // SUB), pots, *into)

    def finish(block, held):
        rows_ref[pl.ds(row_index(block), 1), :] = merge_rows(*held)

    def step(block, is_even):
        finish(block - 1, odd if is_even else even)
        reduce(block, even if is_even else odd)

    reduce(0, even)
    two_by_two(blocks, step)
    finish(blocks - 1, odd)
    repeat(part_ref, rows_ref[...])


def col_kernel(
    count, score_ref, parts_ref, pot_ref, part_ref, peaks, totals, even, odd
):
    merge_parts(parts_ref, count, pot_ref)
    rows, cols = score_ref.shape
    blocks = rows // LANES

    def widen(block, into):
        row = pot_ref[pl.ds(row_index(block), 1), :]
        into[...] = jnp.broadcast_to(row, (LANES, LANES)).T

    def reduce(block, wide):
        here = pl.ds(pl.multiple_of(block * LANES, LANES), LANES)
        there = pl.ds(pl.multiple_of(block * SUB, SUB), SUB)
        pots = wide[...]
        for k in range(cols // LANES):
            lanes = slice(k * LANES, (k + 1) * LANES)
            tile = score_ref[here, lanes] + pots
            tiles = [tile[i : i + SUB] for i in range(0, LANES, SUB)]
            peak = tree(jnp.maximum, tiles)
            peaks[there, lanes] = peak
            totals[there, lanes] = power_sum(tiles, peak)

    def step(block, is_even):
        widen(block, even if is_even else odd)
        reduce(block - 1, odd if is_even else even)

    widen(0, even)
    two_by_two(blocks, step)
    reduce(blocks - 1, odd)
    for k in range(cols // LANES):
        lanes = slice(k * LANES, (k + 1) * LANES)
        part_ref[0, k : k + 1, :] = merge(peaks[:, lanes], totals[:, lanes])
    repeat(part_ref, part_ref[0])


def last_kernel(count, parts_ref, pot_f_ref, src_sq_ref, tgt_sq_ref, out_f_ref, out_g_ref):
    out_f_ref[...] = pot_f_ref[...] * UNIT + src_sq_ref[...]
    merge_parts(parts_ref, count, out_g_ref)
    out_g_ref[...] = out_g_ref[...] * UNIT + tgt_sq_ref[...]


def params():
    return pltpu.CompilerParams(vmem_limit_bytes=VMEM_LIMIT)


def vec(size):
    return jax.ShapeDtypeStruct((size // LANES, LANES), jnp.float32)


def vecs(copies, size):
    return jax.ShapeDtypeStruct((copies, size // LANES, LANES), jnp.float32)


def scratch(*shape):
    return pltpu.VMEM(shape, jnp.float32)


ANYWHERE = pl.BlockSpec(memory_space=pl.ANY)
IN_VMEM = pl.BlockSpec(memory_space=pltpu.VMEM)


def place(own, other, side, side_other, far, theirs, theirs_far, start):
    rows, width = 8 * own.shape[0], own.shape[1]
    return pl.pallas_call(
        place_kernel,
        out_shape=(pltpu.VMEM((width, rows), own.dtype), vec(rows), vec(rows)),
        in_specs=[IN_VMEM] * 8,
        out_specs=(IN_VMEM,) * 3,
        cost_estimate=cost(rows, width, 1),
        compiler_params=params(),
        name="place",
    )(own, other, side, side_other, far, theirs, theirs_far, start)


def bring(*arrays):
    return pl.pallas_call(
        bring_kernel,
        out_shape=tuple(pltpu.VMEM(a.shape, a.dtype) for a in arrays),
        in_specs=[pl.BlockSpec(memory_space=pltpu.HBM)] * len(arrays),
        out_specs=(IN_VMEM,) * len(arrays),
        scratch_shapes=[pltpu.SemaphoreType.DMA] * len(arrays),
        compiler_params=params(),
        name="bring",
    )(*[pltpu.with_memory_space_constraint(a, pltpu.HBM) for a in arrays])


def cost(rows, cols, width):
    return pl.CostEstimate(
        flops=2 * rows * cols * width, bytes_accessed=8 * rows * cols, transcendentals=rows * cols
    )


STEP = 256


def step_scratch():
    return [scratch(LANES, LANES)] * 8


def own_pass(points, targets, pot, rows):
    width, cols = targets.shape
    return pl.pallas_call(
        own_kernel,
        out_shape=(pltpu.VMEM((rows, cols), jnp.float32), vec(rows), vec(rows)),
        in_specs=[IN_VMEM] * 3,
        out_specs=(IN_VMEM,) * 3,
        scratch_shapes=step_scratch(),
        cost_estimate=cost(points.shape[0], cols, width),
        compiler_params=params(),
        name="own_pass",
    )(points, targets, pot)


def more_pass(state, points, blocks, targets, pot, copies):
    score, row_parts, src_sq = state
    (rows, cols), width = score.shape, targets.shape[0]
    added = sum(array.shape[0] for array in points)
    score = pltpu.with_memory_space_constraint(score, pltpu.VMEM)
    return pl.pallas_call(
        functools.partial(more_kernel, blocks),
        out_shape=(pltpu.VMEM((rows, cols), jnp.float32), vecs(copies, rows), vec(rows)),
        in_specs=[IN_VMEM] * (5 + len(points)),
        out_specs=(IN_VMEM,) * 3,
        scratch_shapes=[scratch(rows // LANES, LANES)] + step_scratch(),
        input_output_aliases={0: 0},
        cost_estimate=cost(added, cols, width),
        compiler_params=params(),
        name="more_pass",
    )(score, row_parts, src_sq, targets, pot, *points)


def row_pass_call(score, parts, count, copies):
    rows, cols = score.shape
    return pl.pallas_call(
        functools.partial(row_kernel, count),
        out_shape=vecs(copies, rows),
        in_specs=[IN_VMEM] * 2,
        out_specs=IN_VMEM,
        scratch_shapes=[scratch(cols // LANES, LANES), scratch(rows // LANES, LANES)]
        + [scratch(LANES, LANES)] * 4,
        compiler_params=params(),
        name="row_pass",
    )(score, parts)


def col_pass_call(score, parts, count, copies):
    rows, cols = score.shape
    return pl.pallas_call(
        functools.partial(col_kernel, count),
        out_shape=(pltpu.VMEM((rows // LANES, LANES), jnp.float32), vecs(copies, cols)),
        in_specs=[IN_VMEM] * 2,
        out_specs=(IN_VMEM, IN_VMEM),
        scratch_shapes=[scratch(rows // LANES * SUB, cols)] * 2 + [scratch(LANES, LANES)] * 2,
        compiler_params=params(),
        name="col_pass",
    )(score, parts)


def last_call(parts, pot_f, src_sq, tgt_sq, count):
    return pl.pallas_call(
        functools.partial(last_kernel, count),
        out_shape=(vec(src_sq.size), vec(tgt_sq.size)),
        in_specs=[IN_VMEM] * 4,
        out_specs=(IN_VMEM, IN_VMEM),
        compiler_params=params(),
        name="last",
    )(parts, pltpu.with_memory_space_constraint(pot_f, pltpu.VMEM), src_sq, tgt_sq)


def exchange(part, axis):
    return lax.all_to_all(part, axis, 0, 0, tiled=True)


def move(block, to):
    pairs = []
    for z, core, y, x in itertools.product(range(4), range(2), range(4), range(4)):
        a, b, c, d = to(z, core, y, x)
        pairs.append((((z * 2 + core) * 4 + y) * 4 + x, ((a % 4 * 2 + b) * 4 + c % 4) * 4 + d % 4))
    return lax.ppermute(block, ("src", "tgt"), pairs)


def other_core(block):
    return move(block, lambda z, core, y, x: (z, 1 - core, y, x))


def round_z(block):
    return move(block, lambda z, core, y, x: (z + 1 - 2 * core, core, y, x))


def along_line(block, by):
    return move(block, lambda z, core, y, x: (z, core, y + core * by, x + (1 - core) * by))


def across_lines(block, by):
    return move(block, lambda z, core, y, x: (z, core, y + (1 - core) * by, x + core * by))


def after(value, earlier):
    def kernel(*refs):
        del refs

    return pl.pallas_call(
        kernel,
        out_shape=jax.ShapeDtypeStruct(value.shape, value.dtype),
        in_specs=[ANYWHERE] * 2,
        out_specs=ANYWHERE,
        input_output_aliases={0: 0},
        cost_estimate=pl.CostEstimate(flops=0, bytes_accessed=40_000_000, transcendentals=0),
        compiler_params=params(),
        name="after",
    )(value, earlier)


def gather_targets(own, earlier):
    side = round_z(own)
    other = other_core(own)
    far = round_z(after(side, earlier))
    side_other = round_z(other)
    theirs = other_core(jnp.concatenate([side, side_other]))
    return other, side, side_other, far, theirs, other_core(far)


def local(src_points, tgt_points, tgt_start):
    n_src, n_tgt = lax.axis_size("src"), lax.axis_size("tgt")
    own, size = src_points, src_points.shape[0]
    total_src = size * n_tgt * n_src
    total_tgt = tgt_points.shape[0] * n_src * n_tgt
    held, tgt_held, start = bring(own, tgt_points, tgt_start.reshape(-1, LANES))

    line = jnp.concatenate([held, along_line(own, 2), along_line(own, 1), along_line(own, -1)])
    before, behind = across_lines(line, 1), across_lines(line, -1)
    far = across_lines(before, 1)

    targets, tgt_sq, red_g = place(tgt_held, *gather_targets(tgt_points, line), start)
    targets = pltpu.with_memory_space_constraint(targets, pltpu.VMEM)
    state = own_pass(line, targets, red_g, size * n_tgt)
    for points, block in ((before, 12), (behind, 4)):
        score, part, src_sq = more_pass(state, (points,), (block,), targets, red_g, 1)
        state = score, part[0], src_sq
    score, part, src_sq = more_pass(state, (far,), (8,), targets, red_g, n_tgt)
    score = pltpu.with_memory_space_constraint(score, pltpu.VMEM)
    for step in range(ITERS):
        if step:
            part = row_pass_call(score, parts, total_src, n_tgt)
        parts = exchange(part, "tgt")
        red_f, part = col_pass_call(score, parts, total_tgt, n_src)
        parts = exchange(part, "src")
    pot_f, pot_g = last_call(parts, red_f, src_sq, tgt_sq, total_src)
    return (pot_f.reshape(-1), pot_g.reshape(-1))


def solution(mesh):
    return jax.shard_map(
        local,
        mesh=mesh,
        in_specs=(P(("src", "tgt"), None), P(("tgt", "src"), None), P("tgt")),
        out_specs=(P("src"), P("tgt")),
        check_vma=False,
    )
```

```python
import functools
import itertools
import math

import jax
import jax.numpy as jnp
from jax import lax
from jax.experimental import pallas as pl
from jax.experimental.pallas import tpu as pltpu
from jax.sharding import PartitionSpec as P

ITERS = 2


EPSILON = 0.05
UNIT = EPSILON * math.log(2.0)

LANES = 128
SUB = 8
VMEM_LIMIT = 16 * 1024 * 1024


def tree(op, values):
    values = list(values)
    while len(values) > 1:
        values = [
            op(values[i], values[i + 1]) if i + 1 < len(values) else values[i]
            for i in range(0, len(values), 2)
        ]
    return values[0]


def merge(peaks, totals):
    peak = jnp.max(peaks, axis=0, keepdims=True)
    return peak + jnp.log2(jnp.sum(totals * jnp.exp2(peaks - peak), axis=0, keepdims=True))


def merge_parts(parts_ref, count, out_ref):
    parts = [parts_ref[i] for i in range(parts_ref.shape[0])]
    peak = tree(jnp.maximum, parts)
    total = tree(jnp.add, [jnp.exp2(part - peak) for part in parts])
    out_ref[...] = math.log2(count) - (peak + jnp.log2(total))


def repeat(part_ref, part):
    for copy in range(part_ref.shape[0]):
        part_ref[copy] = part


def power_sum(tiles, peak):
    return tree(jnp.add, [jnp.exp2(tile - peak) for tile in tiles])


def lane_tiles(rows):
    return [rows[:, k : k + LANES] for k in range(0, rows.shape[1], LANES)]


def reduce_rows(score_ref, start, groups, pots, peaks, totals):
    for group in groups:
        rows = pl.ds(start + group * SUB, SUB)
        tiles = [tile + pot for tile, pot in zip(lane_tiles(score_ref[rows, :]), pots)]
        peak = tree(jnp.maximum, tiles)
        at = group * SUB
        peaks[at : at + SUB, :] = peak
        totals[at : at + SUB, :] = power_sum(tiles, peak)


def merge_rows(peaks, totals):
    return merge(peaks[...].T, totals[...].T)


def pot_rows(pot_ref):
    return [
        jnp.broadcast_to(pot_ref[k : k + 1, :], (SUB, LANES)) for k in range(pot_ref.shape[0])
    ]


def squares(points):
    wide = points.astype(jnp.float32)
    return jnp.sum(tree(jnp.add, lane_tiles(wide * wide)).T, axis=0, keepdims=True)


def place_kernel(
    own_ref, other_ref, side_ref, side_other_ref, far_ref, theirs_ref, theirs_far_ref, start_ref, targets, sq_ref, pot_ref
):
    own = lax.axis_index("src")
    core = own % 2
    size = own_ref.shape[0]
    chips = targets.shape[0] // (2 * size)

    def put(points, chip, core):
        index = (own // 2 + chip + chips) % chips * 2 + core
        targets[pl.ds(pl.multiple_of(index * size, size), size), :] = points
        per = size // LANES
        for sub in range(per):
            row = squares(points[sub * LANES : (sub + 1) * LANES])
            sq_ref[pl.ds(index * per + sub, 1), :] = row

    side = 2 * core - 1
    put(own_ref[...], 0, core)
    put(other_ref[...], 0, 1 - core)
    put(side_ref[...], side, core)
    put(side_other_ref[...], side, 1 - core)
    put(far_ref[...], 2, core)
    put(theirs_ref[:size, :], -side, 1 - core)
    put(theirs_ref[size:, :], -side, core)
    put(theirs_far_ref[...], 2, 1 - core)
    pot_ref[...] = (start_ref[...] - sq_ref[...]) * (1.0 / UNIT)


def bring_kernel(*refs):
    count = len(refs) // 3
    copies = [
        pltpu.make_async_copy(refs[i], refs[count + i], refs[2 * count + i]) for i in range(count)
    ]
    for copy in copies:
        copy.start()
    for copy in copies:
        copy.wait()


CHUNK = 1024


def row_index(block):
    own, core = lax.axis_index("tgt"), lax.axis_index("src") % 2
    y, x = own // 4, own % 4
    line, place = y + core * (x - y), x + core * (y - x)
    at = block % 4
    by = at + (at + 3) // 4 + at // 3
    to_line, to_place = (line + block // 4) % 4, (place + by) % 4
    return to_line * (4 - 3 * core) + to_place * (1 + 3 * core)


def block_pipeline(sources, tgt_ref, pot_ref, score_ref, rows_ref, sq_ref, peaks, totals):
    per = STEP // LANES
    chunks = tgt_ref.shape[0] // CHUNK
    pots = pot_rows(pot_ref)

    def product(at, chunk):
        ref, first, block = sources[at]
        points = ref[first : first + STEP, :]
        lanes = slice(chunk * CHUNK, (chunk + 1) * CHUNK)
        score_ref[block * LANES : (block + per) * LANES, lanes] = lax.dot_general(
            points, tgt_ref[lanes, :], (((1,), (1,)), ((), ())), preferred_element_type=jnp.float32
        ) * (2.0 / UNIT)
        if chunk < per:
            row = squares(points[chunk * LANES : (chunk + 1) * LANES])
            sq_ref[pl.ds(row_index(block + chunk), 1), :] = row

    def reduce(at, chunk):
        share = chunks // per
        sub, part = chunk // share, chunk % share
        held = at % 2 * per + sub
        start = (sources[at][2] + sub) * LANES
        size = LANES // SUB // share
        groups = range(part * size, (part + 1) * size)
        reduce_rows(score_ref, start, groups, pots, peaks[held], totals[held])

    def finish(at):
        for sub in range(per):
            held = at % 2 * per + sub
            row = merge_rows(peaks[held], totals[held])
            rows_ref[pl.ds(row_index(sources[at][2] + sub), 1), :] = row

    for chunk in range(chunks):
        product(0, chunk)
    for at in range(len(sources)):
        for chunk in range(chunks):
            if at + 1 < len(sources):
                product(at + 1, chunk)
            reduce(at, chunk)
            if at and chunk == chunks // 2:
                finish(at - 1)
    finish(len(sources) - 1)


def own_kernel(points_ref, tgt_ref, pot_ref, score_ref, rows_ref, src_sq_ref, *held):
    sources = [(points_ref, 0, 0), (points_ref, STEP, 2)]
    block_pipeline(sources, tgt_ref, pot_ref, score_ref, rows_ref, src_sq_ref, held[:4], held[4:])


def more_kernel(
    blocks, score_in_ref, rows_in_ref, src_sq_in_ref, tgt_ref, pot_ref, *refs
):
    point_refs, refs = refs[: len(blocks)], refs[len(blocks) :]
    score_ref, part_ref, src_sq_ref, rows_ref, *held = refs
    rows_ref[...] = rows_in_ref[...]
    src_sq_ref[...] = src_sq_in_ref[...]
    sources = [
        (ref, first, block + first // LANES)
        for ref, block in zip(point_refs, blocks)
        for first in range(0, ref.shape[0], STEP)
    ]
    block_pipeline(sources, tgt_ref, pot_ref, score_ref, rows_ref, src_sq_ref, held[:4], held[4:])
    repeat(part_ref, rows_ref[...])


def two_by_two(blocks, step):
    step(1, False)

    @pl.loop(1, blocks // 2)
    def _(pair):
        step(2 * pair, True)
        step(2 * pair + 1, False)


def row_kernel(count, score_ref, parts_ref, part_ref, pot_ref, rows_ref, *held):
    merge_parts(parts_ref, count, pot_ref)
    pots = pot_rows(pot_ref)
    blocks = score_ref.shape[0] // LANES
    even, odd = held[:2], held[2:]

    def reduce(block, into):
        start = pl.multiple_of(block * LANES, LANES)
        reduce_rows(score_ref, start, range(LANES // SUB), pots, *into)

    def finish(block, held):
        rows_ref[pl.ds(row_index(block), 1), :] = merge_rows(*held)

    def step(block, is_even):
        finish(block - 1, odd if is_even else even)
        reduce(block, even if is_even else odd)

    reduce(0, even)
    two_by_two(blocks, step)
    finish(blocks - 1, odd)
    repeat(part_ref, rows_ref[...])


def col_kernel(
    count, score_ref, parts_ref, pot_ref, part_ref, peaks, totals, even, odd
):
    merge_parts(parts_ref, count, pot_ref)
    rows, cols = score_ref.shape
    blocks = rows // LANES

    def widen(block, into):
        row = pot_ref[pl.ds(row_index(block), 1), :]
        into[...] = jnp.broadcast_to(row, (LANES, LANES)).T

    def reduce(block, wide):
        here = pl.ds(pl.multiple_of(block * LANES, LANES), LANES)
        there = pl.ds(pl.multiple_of(block * SUB, SUB), SUB)
        pots = wide[...]
        for k in range(cols // LANES):
            lanes = slice(k * LANES, (k + 1) * LANES)
            tile = score_ref[here, lanes] + pots
            tiles = [tile[i : i + SUB] for i in range(0, LANES, SUB)]
            peak = tree(jnp.maximum, tiles)
            peaks[there, lanes] = peak
            totals[there, lanes] = power_sum(tiles, peak)

    def step(block, is_even):
        widen(block, even if is_even else odd)
        reduce(block - 1, odd if is_even else even)

    widen(0, even)
    two_by_two(blocks, step)
    reduce(blocks - 1, odd)
    for k in range(cols // LANES):
        lanes = slice(k * LANES, (k + 1) * LANES)
        part_ref[0, k : k + 1, :] = merge(peaks[:, lanes], totals[:, lanes])
    repeat(part_ref, part_ref[0])


def last_kernel(count, parts_ref, pot_f_ref, src_sq_ref, tgt_sq_ref, out_f_ref, out_g_ref):
    out_f_ref[...] = pot_f_ref[...] * UNIT + src_sq_ref[...]
    merge_parts(parts_ref, count, out_g_ref)
    out_g_ref[...] = out_g_ref[...] * UNIT + tgt_sq_ref[...]


def params():
    return pltpu.CompilerParams(vmem_limit_bytes=VMEM_LIMIT)


def vec(size):
    return jax.ShapeDtypeStruct((size // LANES, LANES), jnp.float32)


def vecs(copies, size):
    return jax.ShapeDtypeStruct((copies, size // LANES, LANES), jnp.float32)


def scratch(*shape):
    return pltpu.VMEM(shape, jnp.float32)


ANYWHERE = pl.BlockSpec(memory_space=pl.ANY)
IN_VMEM = pl.BlockSpec(memory_space=pltpu.VMEM)


def place(own, other, side, side_other, far, theirs, theirs_far, start):
    rows, width = 8 * own.shape[0], own.shape[1]
    return pl.pallas_call(
        place_kernel,
        out_shape=(pltpu.VMEM((rows, width), own.dtype), vec(rows), vec(rows)),
        in_specs=[IN_VMEM] * 8,
        out_specs=(IN_VMEM,) * 3,
        cost_estimate=cost(rows, width, 1),
        compiler_params=params(),
        name="place",
    )(own, other, side, side_other, far, theirs, theirs_far, start)


def bring(*arrays):
    return pl.pallas_call(
        bring_kernel,
        out_shape=tuple(pltpu.VMEM(a.shape, a.dtype) for a in arrays),
        in_specs=[pl.BlockSpec(memory_space=pltpu.HBM)] * len(arrays),
        out_specs=(IN_VMEM,) * len(arrays),
        scratch_shapes=[pltpu.SemaphoreType.DMA] * len(arrays),
        compiler_params=params(),
        name="bring",
    )(*[pltpu.with_memory_space_constraint(a, pltpu.HBM) for a in arrays])


def cost(rows, cols, width):
    return pl.CostEstimate(
        flops=2 * rows * cols * width, bytes_accessed=8 * rows * cols, transcendentals=rows * cols
    )


STEP = 256


def step_scratch():
    return [scratch(LANES, LANES)] * 8


def own_pass(points, targets, pot, rows):
    cols, width = targets.shape
    return pl.pallas_call(
        own_kernel,
        out_shape=(pltpu.VMEM((rows, cols), jnp.float32), vec(rows), vec(rows)),
        in_specs=[IN_VMEM] * 3,
        out_specs=(IN_VMEM,) * 3,
        scratch_shapes=step_scratch(),
        cost_estimate=cost(points.shape[0], cols, width),
        compiler_params=params(),
        name="own_pass",
    )(points, targets, pot)


def more_pass(state, points, blocks, targets, pot, copies):
    score, row_parts, src_sq = state
    (rows, cols), width = score.shape, targets.shape[1]
    added = sum(array.shape[0] for array in points)
    score = pltpu.with_memory_space_constraint(score, pltpu.VMEM)
    return pl.pallas_call(
        functools.partial(more_kernel, blocks),
        out_shape=(pltpu.VMEM((rows, cols), jnp.float32), vecs(copies, rows), vec(rows)),
        in_specs=[IN_VMEM] * (5 + len(points)),
        out_specs=(IN_VMEM,) * 3,
        scratch_shapes=[scratch(rows // LANES, LANES)] + step_scratch(),
        input_output_aliases={0: 0},
        cost_estimate=cost(added, cols, width),
        compiler_params=params(),
        name="more_pass",
    )(score, row_parts, src_sq, targets, pot, *points)


def row_pass_call(score, parts, count, copies):
    rows, cols = score.shape
    return pl.pallas_call(
        functools.partial(row_kernel, count),
        out_shape=vecs(copies, rows),
        in_specs=[IN_VMEM] * 2,
        out_specs=IN_VMEM,
        scratch_shapes=[scratch(cols // LANES, LANES), scratch(rows // LANES, LANES)]
        + [scratch(LANES, LANES)] * 4,
        compiler_params=params(),
        name="row_pass",
    )(score, parts)


def col_pass_call(score, parts, count, copies):
    rows, cols = score.shape
    return pl.pallas_call(
        functools.partial(col_kernel, count),
        out_shape=(pltpu.VMEM((rows // LANES, LANES), jnp.float32), vecs(copies, cols)),
        in_specs=[IN_VMEM] * 2,
        out_specs=(IN_VMEM, IN_VMEM),
        scratch_shapes=[scratch(rows // LANES * SUB, cols)] * 2 + [scratch(LANES, LANES)] * 2,
        compiler_params=params(),
        name="col_pass",
    )(score, parts)


def last_call(parts, pot_f, src_sq, tgt_sq, count):
    return pl.pallas_call(
        functools.partial(last_kernel, count),
        out_shape=(vec(src_sq.size), vec(tgt_sq.size)),
        in_specs=[IN_VMEM] * 4,
        out_specs=(IN_VMEM, IN_VMEM),
        compiler_params=params(),
        name="last",
    )(parts, pltpu.with_memory_space_constraint(pot_f, pltpu.VMEM), src_sq, tgt_sq)


def exchange(part, axis):
    return lax.all_to_all(part, axis, 0, 0, tiled=True)


def move(block, to):
    pairs = []
    for z, core, y, x in itertools.product(range(4), range(2), range(4), range(4)):
        a, b, c, d = to(z, core, y, x)
        pairs.append((((z * 2 + core) * 4 + y) * 4 + x, ((a % 4 * 2 + b) * 4 + c % 4) * 4 + d % 4))
    return lax.ppermute(block, ("src", "tgt"), pairs)


def other_core(block):
    return move(block, lambda z, core, y, x: (z, 1 - core, y, x))


def round_z(block):
    return move(block, lambda z, core, y, x: (z + 1 - 2 * core, core, y, x))


def along_line(block, by):
    return move(block, lambda z, core, y, x: (z, core, y + core * by, x + (1 - core) * by))


def across_lines(block, by):
    return move(block, lambda z, core, y, x: (z, core, y + (1 - core) * by, x + core * by))


def after(value, earlier):
    def kernel(*refs):
        del refs

    return pl.pallas_call(
        kernel,
        out_shape=jax.ShapeDtypeStruct(value.shape, value.dtype),
        in_specs=[ANYWHERE] * 2,
        out_specs=ANYWHERE,
        input_output_aliases={0: 0},
        cost_estimate=pl.CostEstimate(flops=0, bytes_accessed=40_000_000, transcendentals=0),
        compiler_params=params(),
        name="after",
    )(value, earlier)


def gather_targets(own, earlier):
    side = round_z(own)
    other = other_core(own)
    far = round_z(after(side, earlier))
    side_other = round_z(other)
    theirs = other_core(jnp.concatenate([side, side_other]))
    return other, side, side_other, far, theirs, other_core(far)


def local(src_points, tgt_points, tgt_start):
    n_src, n_tgt = lax.axis_size("src"), lax.axis_size("tgt")
    own, size = src_points, src_points.shape[0]
    total_src = size * n_tgt * n_src
    total_tgt = tgt_points.shape[0] * n_src * n_tgt
    held, tgt_held, start = bring(own, tgt_points, tgt_start.reshape(-1, LANES))

    line = jnp.concatenate([held, along_line(own, 2), along_line(own, 1), along_line(own, -1)])
    before, behind = across_lines(line, 1), across_lines(line, -1)
    far = across_lines(before, 1)

    targets, tgt_sq, red_g = place(tgt_held, *gather_targets(tgt_points, line), start)
    targets = pltpu.with_memory_space_constraint(targets, pltpu.VMEM)
    state = own_pass(line, targets, red_g, size * n_tgt)
    for points, block in ((before, 12), (behind, 4)):
        score, part, src_sq = more_pass(state, (points,), (block,), targets, red_g, 1)
        state = score, part[0], src_sq
    score, part, src_sq = more_pass(state, (far,), (8,), targets, red_g, n_tgt)
    score = pltpu.with_memory_space_constraint(score, pltpu.VMEM)
    for step in range(ITERS):
        if step:
            part = row_pass_call(score, parts, total_src, n_tgt)
        parts = exchange(part, "tgt")
        red_f, part = col_pass_call(score, parts, total_tgt, n_src)
        parts = exchange(part, "src")
    pot_f, pot_g = last_call(parts, red_f, src_sq, tgt_sq, total_src)
    return (pot_f.reshape(-1), pot_g.reshape(-1))


def solution(mesh):
    return jax.shard_map(
        local,
        mesh=mesh,
        in_specs=(P(("src", "tgt"), None), P(("tgt", "src"), None), P("tgt")),
        out_specs=(P("src"), P("tgt")),
        check_vma=False,
    )
```

```python
import functools
import itertools
import math

import jax
import jax.numpy as jnp
from jax import lax
from jax.experimental import pallas as pl
from jax.experimental.pallas import tpu as pltpu
from jax.sharding import PartitionSpec as P

EPSILON = 0.05
UNIT = EPSILON * math.log(2.0)

LANES = 128
SUB = 8
VMEM_LIMIT = 12 * 1024 * 1024


def tree(op, values):
    values = list(values)
    while len(values) > 1:
        values = [
            op(values[i], values[i + 1]) if i + 1 < len(values) else values[i]
            for i in range(0, len(values), 2)
        ]
    return values[0]


def merge(peaks, totals):
    peak = jnp.max(peaks, axis=0, keepdims=True)
    return peak + jnp.log2(jnp.sum(totals * jnp.exp2(peaks - peak), axis=0, keepdims=True))


def merge_parts(parts_ref, count, out_ref):
    parts = [parts_ref[i] for i in range(parts_ref.shape[0])]
    peak = tree(jnp.maximum, parts)
    total = tree(jnp.add, [jnp.exp2(part - peak) for part in parts])
    out_ref[...] = math.log2(count) - (peak + jnp.log2(total))


def repeat(part_ref, part):
    for copy in range(part_ref.shape[0]):
        part_ref[copy] = part


def power_sum(tiles, peak):
    return tree(jnp.add, [jnp.exp2(tile - peak) for tile in tiles])


def lane_tiles(rows):
    return [rows[:, k : k + LANES] for k in range(0, rows.shape[1], LANES)]


def reduce_rows(score_ref, start, groups, pots, peaks, totals):
    for group in groups:
        rows = pl.ds(start + group * SUB, SUB)
        tiles = [tile + pot for tile, pot in zip(lane_tiles(score_ref[rows, :]), pots)]
        peak = tree(jnp.maximum, tiles)
        at = group * SUB
        peaks[at : at + SUB, :] = peak
        totals[at : at + SUB, :] = power_sum(tiles, peak)


def merge_rows(peaks, totals):
    return merge(peaks[...].T, totals[...].T)


def pot_rows(pot_ref):
    return [
        jnp.broadcast_to(pot_ref[k : k + 1, :], (SUB, LANES)) for k in range(pot_ref.shape[0])
    ]


def squares(points):
    wide = points.astype(jnp.float32)
    return jnp.sum(tree(jnp.add, lane_tiles(wide * wide)).T, axis=0, keepdims=True)


def place_kernel(
    own_ref, other_ref, side_ref, side_other_ref, far_ref, theirs_ref, theirs_far_ref, start_ref, targets, sq_ref, pot_ref
):
    own = lax.axis_index("src")
    core = own % 2
    size = own_ref.shape[0]
    chips = targets.shape[0] // (2 * size)

    def put(points, chip, core):
        index = (own // 2 + chip + chips) % chips * 2 + core
        targets[pl.ds(pl.multiple_of(index * size, size), size), :] = points
        per = size // LANES
        for sub in range(per):
            row = squares(points[sub * LANES : (sub + 1) * LANES])
            sq_ref[pl.ds(index * per + sub, 1), :] = row

    side = 2 * core - 1
    put(own_ref[...], 0, core)
    put(other_ref[...], 0, 1 - core)
    put(side_ref[...], side, core)
    put(side_other_ref[...], side, 1 - core)
    put(far_ref[...], 2, core)
    put(theirs_ref[:size, :], -side, 1 - core)
    put(theirs_ref[size:, :], -side, core)
    put(theirs_far_ref[...], 2, 1 - core)
    pot_ref[...] = (start_ref[...] - sq_ref[...]) * (1.0 / UNIT)


def bring_kernel(*refs):
    count = len(refs) // 3
    copies = [
        pltpu.make_async_copy(refs[i], refs[count + i], refs[2 * count + i]) for i in range(count)
    ]
    for copy in copies:
        copy.start()
    for copy in copies:
        copy.wait()


CHUNK = 1024


def row_index(block):
    own, core = lax.axis_index("tgt"), lax.axis_index("src") % 2
    y, x = own // 4, own % 4
    line, place = y + core * (x - y), x + core * (y - x)
    at = block % 4
    by = at + (at + 3) // 4 + at // 3
    to_line, to_place = (line + block // 4) % 4, (place + by) % 4
    return to_line * (4 - 3 * core) + to_place * (1 + 3 * core)


def block_pipeline(sources, tgt_ref, pot_ref, score_ref, rows_ref, sq_ref, peaks, totals):
    per = STEP // LANES
    chunks = tgt_ref.shape[0] // CHUNK
    pots = pot_rows(pot_ref)

    def product(at, chunk):
        ref, first, block = sources[at]
        points = ref[first : first + STEP, :]
        lanes = slice(chunk * CHUNK, (chunk + 1) * CHUNK)
        score_ref[block * LANES : (block + per) * LANES, lanes] = lax.dot_general(
            points, tgt_ref[lanes, :], (((1,), (1,)), ((), ())), preferred_element_type=jnp.float32
        ) * (2.0 / UNIT)
        if chunk < per:
            row = squares(points[chunk * LANES : (chunk + 1) * LANES])
            sq_ref[pl.ds(row_index(block + chunk), 1), :] = row

    def reduce(at, chunk):
        share = chunks // per
        sub, part = chunk // share, chunk % share
        held = at % 2 * per + sub
        start = (sources[at][2] + sub) * LANES
        size = LANES // SUB // share
        groups = range(part * size, (part + 1) * size)
        reduce_rows(score_ref, start, groups, pots, peaks[held], totals[held])

    def finish(at):
        for sub in range(per):
            held = at % 2 * per + sub
            row = merge_rows(peaks[held], totals[held])
            rows_ref[pl.ds(row_index(sources[at][2] + sub), 1), :] = row

    for chunk in range(chunks):
        product(0, chunk)
    for at in range(len(sources)):
        for chunk in range(chunks):
            if at + 1 < len(sources):
                product(at + 1, chunk)
            reduce(at, chunk)
            if at and chunk == chunks // 2:
                finish(at - 1)
    finish(len(sources) - 1)


def own_kernel(points_ref, tgt_ref, pot_ref, score_ref, rows_ref, src_sq_ref, *held):
    sources = [(points_ref, 0, 0), (points_ref, STEP, 2)]
    block_pipeline(sources, tgt_ref, pot_ref, score_ref, rows_ref, src_sq_ref, held[:4], held[4:])


def more_kernel(
    blocks, score_in_ref, rows_in_ref, src_sq_in_ref, tgt_ref, pot_ref, *refs
):
    point_refs, refs = refs[: len(blocks)], refs[len(blocks) :]
    score_ref, part_ref, src_sq_ref, rows_ref, *held = refs
    rows_ref[...] = rows_in_ref[...]
    src_sq_ref[...] = src_sq_in_ref[...]
    sources = [
        (ref, first, block + first // LANES)
        for ref, block in zip(point_refs, blocks)
        for first in range(0, ref.shape[0], STEP)
    ]
    block_pipeline(sources, tgt_ref, pot_ref, score_ref, rows_ref, src_sq_ref, held[:4], held[4:])
    repeat(part_ref, rows_ref[...])


def two_by_two(blocks, step):
    step(1, False)

    @pl.loop(1, blocks // 2)
    def _(pair):
        step(2 * pair, True)
        step(2 * pair + 1, False)


def row_kernel(count, score_ref, parts_ref, part_ref, pot_ref, rows_ref, *held):
    merge_parts(parts_ref, count, pot_ref)
    pots = pot_rows(pot_ref)
    blocks = score_ref.shape[0] // LANES
    even, odd = held[:2], held[2:]

    def reduce(block, into):
        start = pl.multiple_of(block * LANES, LANES)
        reduce_rows(score_ref, start, range(LANES // SUB), pots, *into)

    def finish(block, held):
        rows_ref[pl.ds(row_index(block), 1), :] = merge_rows(*held)

    def step(block, is_even):
        finish(block - 1, odd if is_even else even)
        reduce(block, even if is_even else odd)

    reduce(0, even)
    two_by_two(blocks, step)
    finish(blocks - 1, odd)
    repeat(part_ref, rows_ref[...])


def by_row_blocks(pot_ref, blocks, reduce, even, odd):
    def widen(block, into):
        row = pot_ref[pl.ds(row_index(block), 1), :]
        into[...] = jnp.broadcast_to(row, (LANES, LANES)).T

    def run(block, wide):
        here = pl.ds(pl.multiple_of(block * LANES, LANES), LANES)
        there = pl.ds(pl.multiple_of(block * SUB, SUB), SUB)
        reduce(here, there, wide[...])

    def step(block, is_even):
        widen(block, even if is_even else odd)
        run(block - 1, odd if is_even else even)

    widen(0, even)
    two_by_two(blocks, step)
    run(blocks - 1, odd)


def column_tiles(cols):
    return [slice(k, k + LANES) for k in range(0, cols, LANES)]


def row_groups(tile):
    return [tile[i : i + SUB] for i in range(0, LANES, SUB)]


def exact_columns(score_ref, pot_ref, part_ref, peaks, totals, even, odd, table_ref=None):
    rows, cols = score_ref.shape

    def reduce(here, there, pots):
        for lanes in column_tiles(cols):
            tiles = row_groups(score_ref[here, lanes] + pots)
            peak = tree(jnp.maximum, tiles)
            powers = [jnp.exp2(tile - peak) for tile in tiles]
            peaks[there, lanes] = peak
            totals[there, lanes] = tree(jnp.add, powers)
            if table_ref is not None:
                table_ref[here, lanes] = jnp.concatenate(powers, axis=0).astype(jnp.bfloat16)

    by_row_blocks(pot_ref, rows // LANES, reduce, even, odd)
    for k, lanes in enumerate(column_tiles(cols)):
        part_ref[0, k : k + 1, :] = merge(peaks[:, lanes], totals[:, lanes])


def col_kernel(
    count, score_ref, parts_ref, pot_ref, part_ref, table_ref, peaks, totals, even, odd
):
    merge_parts(parts_ref, count, pot_ref)
    exact_columns(score_ref, pot_ref, part_ref, peaks, totals, even, odd, table_ref)
    repeat(part_ref, part_ref[0])


FLOOR = 1e-28
LARGEST = 1e30


def last_col_kernel(
    count, score_ref, parts_ref, table_ref, kept_ref, before_ref, pot_ref, part_ref,
    ratio_ref, peaks, totals, even, odd,
):
    merge_parts(parts_ref, count, pot_ref)
    ratio = jnp.exp2(pot_ref[...] - before_ref[...])
    ratio_ref[...] = ratio
    rows, cols = score_ref.shape

    def reduce(here, there, weights):
        for lanes in column_tiles(cols):
            tile = table_ref[here, lanes].astype(jnp.float32) * weights
            totals[there, lanes] = tree(jnp.add, row_groups(tile))

    by_row_blocks(ratio_ref, rows // LANES, reduce, even, odd)
    sums = []
    for k, lanes in enumerate(column_tiles(cols)):
        peak = jnp.max(kept_ref[:, lanes], axis=0, keepdims=True)
        scaled = totals[:, lanes] * jnp.exp2(kept_ref[:, lanes] - peak)
        sums.append(jnp.sum(scaled, axis=0, keepdims=True))
        part_ref[0, k : k + 1, :] = peak + jnp.log2(sums[-1])

    largest, least = jnp.max(ratio), jnp.min(tree(jnp.minimum, sums))
    whole = (largest <= LARGEST) & (least >= FLOOR * jnp.maximum(largest, 1.0))

    @pl.when(jnp.logical_not(whole))
    def _():
        exact_columns(score_ref, pot_ref, part_ref, peaks, totals, even, odd)

    repeat(part_ref, part_ref[0])


def last_kernel(count, parts_ref, pot_f_ref, src_sq_ref, tgt_sq_ref, out_f_ref, out_g_ref):
    out_f_ref[...] = pot_f_ref[...] * UNIT + src_sq_ref[...]
    merge_parts(parts_ref, count, out_g_ref)
    out_g_ref[...] = out_g_ref[...] * UNIT + tgt_sq_ref[...]


def params():
    return pltpu.CompilerParams(vmem_limit_bytes=VMEM_LIMIT)


def vec(size):
    return jax.ShapeDtypeStruct((size // LANES, LANES), jnp.float32)


def vecs(copies, size):
    return jax.ShapeDtypeStruct((copies, size // LANES, LANES), jnp.float32)


def scratch(*shape):
    return pltpu.VMEM(shape, jnp.float32)


ANYWHERE = pl.BlockSpec(memory_space=pl.ANY)
IN_VMEM = pl.BlockSpec(memory_space=pltpu.VMEM)


def place(own, other, side, side_other, far, theirs, theirs_far, start):
    rows, width = 8 * own.shape[0], own.shape[1]
    return pl.pallas_call(
        place_kernel,
        out_shape=(pltpu.VMEM((rows, width), own.dtype), vec(rows), vec(rows)),
        in_specs=[IN_VMEM] * 8,
        out_specs=(IN_VMEM,) * 3,
        cost_estimate=cost(rows, width, 1),
        compiler_params=params(),
        name="place",
    )(own, other, side, side_other, far, theirs, theirs_far, start)


def bring(*arrays):
    return pl.pallas_call(
        bring_kernel,
        out_shape=tuple(pltpu.VMEM(a.shape, a.dtype) for a in arrays),
        in_specs=[pl.BlockSpec(memory_space=pltpu.HBM)] * len(arrays),
        out_specs=(IN_VMEM,) * len(arrays),
        scratch_shapes=[pltpu.SemaphoreType.DMA] * len(arrays),
        compiler_params=params(),
        name="bring",
    )(*[pltpu.with_memory_space_constraint(a, pltpu.HBM) for a in arrays])


def cost(rows, cols, width):
    return pl.CostEstimate(
        flops=2 * rows * cols * width, bytes_accessed=8 * rows * cols, transcendentals=rows * cols
    )


STEP = 256


def step_scratch():
    return [scratch(LANES, LANES)] * 8


def own_pass(points, targets, pot, rows):
    cols, width = targets.shape
    return pl.pallas_call(
        own_kernel,
        out_shape=(pltpu.VMEM((rows, cols), jnp.float32), vec(rows), vec(rows)),
        in_specs=[IN_VMEM] * 3,
        out_specs=(IN_VMEM,) * 3,
        scratch_shapes=step_scratch(),
        cost_estimate=cost(points.shape[0], cols, width),
        compiler_params=params(),
        name="own_pass",
    )(points, targets, pot)


def more_pass(state, points, blocks, targets, pot, copies):
    score, row_parts, src_sq = state
    (rows, cols), width = score.shape, targets.shape[1]
    added = sum(array.shape[0] for array in points)
    score = pltpu.with_memory_space_constraint(score, pltpu.VMEM)
    return pl.pallas_call(
        functools.partial(more_kernel, blocks),
        out_shape=(pltpu.VMEM((rows, cols), jnp.float32), vecs(copies, rows), vec(rows)),
        in_specs=[IN_VMEM] * (5 + len(points)),
        out_specs=(IN_VMEM,) * 3,
        scratch_shapes=[scratch(rows // LANES, LANES)] + step_scratch(),
        input_output_aliases={0: 0},
        cost_estimate=cost(added, cols, width),
        compiler_params=params(),
        name="more_pass",
    )(score, row_parts, src_sq, targets, pot, *points)


def row_pass_call(score, parts, count, copies):
    rows, cols = score.shape
    return pl.pallas_call(
        functools.partial(row_kernel, count),
        out_shape=vecs(copies, rows),
        in_specs=[IN_VMEM] * 2,
        out_specs=IN_VMEM,
        scratch_shapes=[scratch(cols // LANES, LANES), scratch(rows // LANES, LANES)]
        + [scratch(LANES, LANES)] * 4,
        compiler_params=params(),
        name="row_pass",
    )(score, parts)


def in_vmem(*arrays):
    return [pltpu.with_memory_space_constraint(array, pltpu.VMEM) for array in arrays]


def col_pass_call(score, parts, count, copies):
    rows, cols = score.shape
    kept = (rows // LANES * SUB, cols)
    red_f, part, *table = pl.pallas_call(
        functools.partial(col_kernel, count),
        out_shape=(
            pltpu.VMEM((rows // LANES, LANES), jnp.float32),
            vecs(copies, cols),
            pltpu.VMEM((rows, cols), jnp.bfloat16),
            pltpu.VMEM(kept, jnp.float32),
        ),
        in_specs=[IN_VMEM] * 2,
        out_specs=(IN_VMEM,) * 4,
        scratch_shapes=[scratch(*kept)] + [scratch(LANES, LANES)] * 2,
        compiler_params=params(),
        name="col_pass",
    )(*in_vmem(score), parts)
    return red_f, part, table


def last_col_call(score, parts, table, before, count, copies):
    rows, cols = score.shape
    return pl.pallas_call(
        functools.partial(last_col_kernel, count),
        out_shape=(pltpu.VMEM((rows // LANES, LANES), jnp.float32), vecs(copies, cols)),
        in_specs=[IN_VMEM] * 5,
        out_specs=(IN_VMEM, IN_VMEM),
        scratch_shapes=[scratch(rows // LANES, LANES)]
        + [scratch(rows // LANES * SUB, cols)] * 2
        + [scratch(LANES, LANES)] * 2,
        compiler_params=params(),
        name="last_col_pass",
    )(*in_vmem(score), parts, *in_vmem(*table, before))


def last_call(parts, pot_f, src_sq, tgt_sq, count):
    return pl.pallas_call(
        functools.partial(last_kernel, count),
        out_shape=(vec(src_sq.size), vec(tgt_sq.size)),
        in_specs=[IN_VMEM] * 4,
        out_specs=(IN_VMEM, IN_VMEM),
        compiler_params=params(),
        name="last",
    )(parts, pltpu.with_memory_space_constraint(pot_f, pltpu.VMEM), src_sq, tgt_sq)


def exchange(part, axis):
    return lax.all_to_all(part, axis, 0, 0, tiled=True)


def move(block, to):
    pairs = []
    for z, core, y, x in itertools.product(range(4), range(2), range(4), range(4)):
        a, b, c, d = to(z, core, y, x)
        pairs.append((((z * 2 + core) * 4 + y) * 4 + x, ((a % 4 * 2 + b) * 4 + c % 4) * 4 + d % 4))
    return lax.ppermute(block, ("src", "tgt"), pairs)


def other_core(block):
    return move(block, lambda z, core, y, x: (z, 1 - core, y, x))


def round_z(block):
    return move(block, lambda z, core, y, x: (z + 1 - 2 * core, core, y, x))


def along_line(block, by):
    return move(block, lambda z, core, y, x: (z, core, y + core * by, x + (1 - core) * by))


def across_lines(block, by):
    return move(block, lambda z, core, y, x: (z, core, y + (1 - core) * by, x + core * by))


def after(value, earlier):
    def kernel(*refs):
        del refs

    return pl.pallas_call(
        kernel,
        out_shape=jax.ShapeDtypeStruct(value.shape, value.dtype),
        in_specs=[ANYWHERE] * 2,
        out_specs=ANYWHERE,
        input_output_aliases={0: 0},
        cost_estimate=pl.CostEstimate(flops=0, bytes_accessed=40_000_000, transcendentals=0),
        compiler_params=params(),
        name="after",
    )(value, earlier)


def gather_targets(own, earlier):
    side = round_z(own)
    other = other_core(own)
    far = round_z(after(side, earlier))
    side_other = round_z(other)
    theirs = other_core(jnp.concatenate([side, side_other]))
    return other, side, side_other, far, theirs, other_core(far)


def local(src_points, tgt_points, tgt_start):
    n_src, n_tgt = lax.axis_size("src"), lax.axis_size("tgt")
    own, size = src_points, src_points.shape[0]
    total_src = size * n_tgt * n_src
    total_tgt = tgt_points.shape[0] * n_src * n_tgt
    held, tgt_held, start = bring(own, tgt_points, tgt_start.reshape(-1, LANES))

    line = jnp.concatenate([held, along_line(own, 2), along_line(own, 1), along_line(own, -1)])
    before, behind = across_lines(line, 1), across_lines(line, -1)
    far = across_lines(before, 1)

    targets, tgt_sq, red_g = place(tgt_held, *gather_targets(tgt_points, line), start)
    targets = pltpu.with_memory_space_constraint(targets, pltpu.VMEM)
    state = own_pass(line, targets, red_g, size * n_tgt)
    for points, block in ((before, 12), (behind, 4)):
        score, part, src_sq = more_pass(state, (points,), (block,), targets, red_g, 1)
        state = score, part[0], src_sq
    score, part, src_sq = more_pass(state, (far,), (8,), targets, red_g, n_tgt)
    score = pltpu.with_memory_space_constraint(score, pltpu.VMEM)
    parts = exchange(part, "tgt")
    first_f, part, table = col_pass_call(score, parts, total_tgt, n_src)
    parts = exchange(part, "src")
    part = row_pass_call(score, parts, total_src, n_tgt)
    parts = exchange(part, "tgt")
    red_f, part = last_col_call(score, parts, table, first_f, total_tgt, n_src)
    parts = exchange(part, "src")
    pot_f, pot_g = last_call(parts, red_f, src_sq, tgt_sq, total_src)
    return (pot_f.reshape(-1), pot_g.reshape(-1))


def solution(mesh):
    return jax.shard_map(
        local,
        mesh=mesh,
        in_specs=(P(("src", "tgt"), None), P(("tgt", "src"), None), P("tgt")),
        out_specs=(P("src"), P("tgt")),
        check_vma=False,
    )
```

```python
import functools
import itertools
import math

import jax
import jax.numpy as jnp
from jax import lax
from jax.experimental import pallas as pl
from jax.experimental.pallas import tpu as pltpu
from jax.sharding import PartitionSpec as P

EPSILON = 0.05
UNIT = EPSILON * math.log(2.0)

LANES = 128
SUB = 8
VMEM_LIMIT = 12 * 1024 * 1024


def tree(op, values):
    values = list(values)
    while len(values) > 1:
        values = [
            op(values[i], values[i + 1]) if i + 1 < len(values) else values[i]
            for i in range(0, len(values), 2)
        ]
    return values[0]


def merge(peaks, totals):
    peak = jnp.max(peaks, axis=0, keepdims=True)
    return peak + jnp.log2(jnp.sum(totals * jnp.exp2(peaks - peak), axis=0, keepdims=True))


def merge_parts(parts_ref, count, out_ref):
    parts = [parts_ref[i] for i in range(parts_ref.shape[0])]
    peak = tree(jnp.maximum, parts)
    total = tree(jnp.add, [jnp.exp2(part - peak) for part in parts])
    out_ref[...] = math.log2(count) - (peak + jnp.log2(total))


def repeat(part_ref, part):
    for copy in range(part_ref.shape[0]):
        part_ref[copy] = part


def power_sum(tiles, peak):
    return tree(jnp.add, [jnp.exp2(tile - peak) for tile in tiles])


def lane_tiles(rows):
    return [rows[:, k : k + LANES] for k in range(0, rows.shape[1], LANES)]


def reduce_rows(score_ref, start, groups, pots, peaks, totals):
    for group in groups:
        rows = pl.ds(start + group * SUB, SUB)
        tiles = [tile + pot for tile, pot in zip(lane_tiles(score_ref[rows, :]), pots)]
        peak = tree(jnp.maximum, tiles)
        at = group * SUB
        peaks[at : at + SUB, :] = peak
        totals[at : at + SUB, :] = power_sum(tiles, peak)


def merge_rows(peaks, totals):
    return merge(peaks[...].T, totals[...].T)


def pot_rows(pot_ref):
    return [
        jnp.broadcast_to(pot_ref[k : k + 1, :], (SUB, LANES)) for k in range(pot_ref.shape[0])
    ]


def squares(points):
    wide = points.astype(jnp.float32)
    return jnp.sum(tree(jnp.add, lane_tiles(wide * wide)).T, axis=0, keepdims=True)


def place_kernel(
    own_ref, other_ref, side_ref, side_other_ref, far_ref, theirs_ref, theirs_other_ref, theirs_far_ref, start_ref, targets, sq_ref, pot_ref
):
    own = lax.axis_index("src")
    core = own % 2
    size = own_ref.shape[0]
    chips = targets.shape[0] // (2 * size)

    def put(points, chip, core):
        index = (own // 2 + chip + chips) % chips * 2 + core
        targets[pl.ds(pl.multiple_of(index * size, size), size), :] = points
        per = size // LANES
        for sub in range(per):
            row = squares(points[sub * LANES : (sub + 1) * LANES])
            sq_ref[pl.ds(index * per + sub, 1), :] = row

    side = 2 * core - 1
    put(own_ref[...], 0, core)
    put(other_ref[...], 0, 1 - core)
    put(side_ref[...], side, core)
    put(side_other_ref[...], side, 1 - core)
    put(far_ref[...], 2, core)
    put(theirs_ref[...], -side, 1 - core)
    put(theirs_other_ref[...], -side, core)
    put(theirs_far_ref[...], 2, 1 - core)
    pot_ref[...] = (start_ref[...] - sq_ref[...]) * (1.0 / UNIT)


def bring_kernel(*refs):
    count = len(refs) // 3
    copies = [
        pltpu.make_async_copy(refs[i], refs[count + i], refs[2 * count + i]) for i in range(count)
    ]
    for copy in copies:
        copy.start()
    for copy in copies:
        copy.wait()


CHUNK = 1024


def row_index(block):
    own, core = lax.axis_index("tgt"), lax.axis_index("src") % 2
    y, x = own // 4, own % 4
    line, place = y + core * (x - y), x + core * (y - x)
    at = block % 4
    by = at + (at + 3) // 4 + at // 3
    to_line, to_place = (line + block // 4) % 4, (place + by) % 4
    return to_line * (4 - 3 * core) + to_place * (1 + 3 * core)


def block_pipeline(sources, tgt_ref, pot_ref, score_ref, rows_ref, sq_ref, peaks, totals):
    per = STEP // LANES
    chunks = tgt_ref.shape[0] // CHUNK
    pots = pot_rows(pot_ref)

    def product(at, chunk):
        ref, first, block = sources[at]
        points = ref[first : first + STEP, :]
        lanes = slice(chunk * CHUNK, (chunk + 1) * CHUNK)
        score_ref[block * LANES : (block + per) * LANES, lanes] = lax.dot_general(
            points, tgt_ref[lanes, :], (((1,), (1,)), ((), ())), preferred_element_type=jnp.float32
        ) * (2.0 / UNIT)
        if chunk < per:
            row = squares(points[chunk * LANES : (chunk + 1) * LANES])
            sq_ref[pl.ds(row_index(block + chunk), 1), :] = row

    def reduce(at, chunk):
        share = chunks // per
        sub, part = chunk // share, chunk % share
        held = at % 2 * per + sub
        start = (sources[at][2] + sub) * LANES
        size = LANES // SUB // share
        groups = range(part * size, (part + 1) * size)
        reduce_rows(score_ref, start, groups, pots, peaks[held], totals[held])

    def finish(at):
        for sub in range(per):
            held = at % 2 * per + sub
            row = merge_rows(peaks[held], totals[held])
            rows_ref[pl.ds(row_index(sources[at][2] + sub), 1), :] = row

    for chunk in range(chunks):
        product(0, chunk)
    for at in range(len(sources)):
        for chunk in range(chunks):
            if at + 1 < len(sources):
                product(at + 1, chunk)
            reduce(at, chunk)
            if at and chunk == chunks // 2:
                finish(at - 1)
    finish(len(sources) - 1)


def own_kernel(points_ref, tgt_ref, pot_ref, score_ref, rows_ref, src_sq_ref, *held):
    sources = [(points_ref, 0, 0), (points_ref, STEP, 2)]
    block_pipeline(sources, tgt_ref, pot_ref, score_ref, rows_ref, src_sq_ref, held[:4], held[4:])


def more_kernel(
    blocks, score_in_ref, rows_in_ref, src_sq_in_ref, tgt_ref, pot_ref, *refs
):
    point_refs, refs = refs[: len(blocks)], refs[len(blocks) :]
    score_ref, part_ref, src_sq_ref, rows_ref, *held = refs
    rows_ref[...] = rows_in_ref[...]
    src_sq_ref[...] = src_sq_in_ref[...]
    sources = [
        (ref, first, block + first // LANES)
        for ref, block in zip(point_refs, blocks)
        for first in range(0, ref.shape[0], STEP)
    ]
    block_pipeline(sources, tgt_ref, pot_ref, score_ref, rows_ref, src_sq_ref, held[:4], held[4:])
    repeat(part_ref, rows_ref[...])


def two_by_two(blocks, step):
    step(1, False)

    @pl.loop(1, blocks // 2)
    def _(pair):
        step(2 * pair, True)
        step(2 * pair + 1, False)


def row_kernel(count, score_ref, parts_ref, part_ref, pot_ref, rows_ref, *held):
    merge_parts(parts_ref, count, pot_ref)
    pots = pot_rows(pot_ref)
    blocks = score_ref.shape[0] // LANES
    even, odd = held[:2], held[2:]

    def reduce(block, into):
        start = pl.multiple_of(block * LANES, LANES)
        reduce_rows(score_ref, start, range(LANES // SUB), pots, *into)

    def finish(block, held):
        rows_ref[pl.ds(row_index(block), 1), :] = merge_rows(*held)

    def step(block, is_even):
        finish(block - 1, odd if is_even else even)
        reduce(block, even if is_even else odd)

    reduce(0, even)
    two_by_two(blocks, step)
    finish(blocks - 1, odd)
    repeat(part_ref, rows_ref[...])


def by_row_blocks(pot_ref, blocks, reduce, even, odd):
    def widen(block, into):
        row = pot_ref[pl.ds(row_index(block), 1), :]
        into[...] = jnp.broadcast_to(row, (LANES, LANES)).T

    def run(block, wide):
        here = pl.ds(pl.multiple_of(block * LANES, LANES), LANES)
        there = pl.ds(pl.multiple_of(block * SUB, SUB), SUB)
        reduce(here, there, wide[...])

    def step(block, is_even):
        widen(block, even if is_even else odd)
        run(block - 1, odd if is_even else even)

    widen(0, even)
    two_by_two(blocks, step)
    run(blocks - 1, odd)


def column_tiles(cols):
    return [slice(k, k + LANES) for k in range(0, cols, LANES)]


def row_groups(tile):
    return [tile[i : i + SUB] for i in range(0, LANES, SUB)]


def exact_columns(score_ref, pot_ref, part_ref, peaks, totals, even, odd, table_ref=None):
    rows, cols = score_ref.shape

    def reduce(here, there, pots):
        for lanes in column_tiles(cols):
            tiles = row_groups(score_ref[here, lanes] + pots)
            peak = tree(jnp.maximum, tiles)
            powers = [jnp.exp2(tile - peak) for tile in tiles]
            peaks[there, lanes] = peak
            totals[there, lanes] = tree(jnp.add, powers)
            if table_ref is not None:
                table_ref[here, lanes] = jnp.concatenate(powers, axis=0).astype(jnp.bfloat16)

    by_row_blocks(pot_ref, rows // LANES, reduce, even, odd)
    for k, lanes in enumerate(column_tiles(cols)):
        part_ref[0, k : k + 1, :] = merge(peaks[:, lanes], totals[:, lanes])


def col_kernel(
    count, score_ref, parts_ref, pot_ref, part_ref, table_ref, peaks, totals, even, odd
):
    merge_parts(parts_ref, count, pot_ref)
    exact_columns(score_ref, pot_ref, part_ref, peaks, totals, even, odd, table_ref)
    repeat(part_ref, part_ref[0])


FLOOR = 1e-28
LARGEST = 1e30


def last_col_kernel(
    count, score_ref, parts_ref, table_ref, kept_ref, before_ref, pot_ref, part_ref,
    ratio_ref, peaks, totals, even, odd,
):
    merge_parts(parts_ref, count, pot_ref)
    ratio = jnp.exp2(pot_ref[...] - before_ref[...])
    ratio_ref[...] = ratio
    rows, cols = score_ref.shape

    def reduce(here, there, weights):
        for lanes in column_tiles(cols):
            tile = table_ref[here, lanes].astype(jnp.float32) * weights
            totals[there, lanes] = tree(jnp.add, row_groups(tile))

    by_row_blocks(ratio_ref, rows // LANES, reduce, even, odd)
    sums = []
    for k, lanes in enumerate(column_tiles(cols)):
        peak = jnp.max(kept_ref[:, lanes], axis=0, keepdims=True)
        scaled = totals[:, lanes] * jnp.exp2(kept_ref[:, lanes] - peak)
        sums.append(jnp.sum(scaled, axis=0, keepdims=True))
        part_ref[0, k : k + 1, :] = peak + jnp.log2(sums[-1])

    largest, least = jnp.max(ratio), jnp.min(tree(jnp.minimum, sums))
    whole = (largest <= LARGEST) & (least >= FLOOR * jnp.maximum(largest, 1.0))

    @pl.when(jnp.logical_not(whole))
    def _():
        exact_columns(score_ref, pot_ref, part_ref, peaks, totals, even, odd)

    repeat(part_ref, part_ref[0])


def last_kernel(count, parts_ref, pot_f_ref, src_sq_ref, tgt_sq_ref, out_f_ref, out_g_ref):
    out_f_ref[...] = pot_f_ref[...] * UNIT + src_sq_ref[...]
    merge_parts(parts_ref, count, out_g_ref)
    out_g_ref[...] = out_g_ref[...] * UNIT + tgt_sq_ref[...]


def params():
    return pltpu.CompilerParams(vmem_limit_bytes=VMEM_LIMIT)


def vec(size):
    return jax.ShapeDtypeStruct((size // LANES, LANES), jnp.float32)


def vecs(copies, size):
    return jax.ShapeDtypeStruct((copies, size // LANES, LANES), jnp.float32)


def scratch(*shape):
    return pltpu.VMEM(shape, jnp.float32)


ANYWHERE = pl.BlockSpec(memory_space=pl.ANY)
IN_VMEM = pl.BlockSpec(memory_space=pltpu.VMEM)


def place(own, other, side, side_other, far, theirs, theirs_other, theirs_far, start):
    rows, width = 8 * own.shape[0], own.shape[1]
    return pl.pallas_call(
        place_kernel,
        out_shape=(pltpu.VMEM((rows, width), own.dtype), vec(rows), vec(rows)),
        in_specs=[IN_VMEM] * 9,
        out_specs=(IN_VMEM,) * 3,
        cost_estimate=cost(rows, width, 1),
        compiler_params=params(),
        name="place",
    )(own, other, side, side_other, far, theirs, theirs_other, theirs_far, start)


def bring(*arrays):
    return pl.pallas_call(
        bring_kernel,
        out_shape=tuple(pltpu.VMEM(a.shape, a.dtype) for a in arrays),
        in_specs=[pl.BlockSpec(memory_space=pltpu.HBM)] * len(arrays),
        out_specs=(IN_VMEM,) * len(arrays),
        scratch_shapes=[pltpu.SemaphoreType.DMA] * len(arrays),
        compiler_params=params(),
        name="bring",
    )(*[pltpu.with_memory_space_constraint(a, pltpu.HBM) for a in arrays])


def cost(rows, cols, width):
    return pl.CostEstimate(
        flops=2 * rows * cols * width, bytes_accessed=8 * rows * cols, transcendentals=rows * cols
    )


STEP = 256


def step_scratch():
    return [scratch(LANES, LANES)] * 8


def own_pass(points, targets, pot, rows):
    cols, width = targets.shape
    return pl.pallas_call(
        own_kernel,
        out_shape=(pltpu.VMEM((rows, cols), jnp.float32), vec(rows), vec(rows)),
        in_specs=[IN_VMEM] * 3,
        out_specs=(IN_VMEM,) * 3,
        scratch_shapes=step_scratch(),
        cost_estimate=cost(points.shape[0], cols, width),
        compiler_params=params(),
        name="own_pass",
    )(points, targets, pot)


def more_pass(state, points, blocks, targets, pot, copies):
    score, row_parts, src_sq = state
    (rows, cols), width = score.shape, targets.shape[1]
    added = sum(array.shape[0] for array in points)
    score = pltpu.with_memory_space_constraint(score, pltpu.VMEM)
    return pl.pallas_call(
        functools.partial(more_kernel, blocks),
        out_shape=(pltpu.VMEM((rows, cols), jnp.float32), vecs(copies, rows), vec(rows)),
        in_specs=[IN_VMEM] * (5 + len(points)),
        out_specs=(IN_VMEM,) * 3,
        scratch_shapes=[scratch(rows // LANES, LANES)] + step_scratch(),
        input_output_aliases={0: 0},
        cost_estimate=cost(added, cols, width),
        compiler_params=params(),
        name="more_pass",
    )(score, row_parts, src_sq, targets, pot, *points)


def row_pass_call(score, parts, count, copies):
    rows, cols = score.shape
    return pl.pallas_call(
        functools.partial(row_kernel, count),
        out_shape=vecs(copies, rows),
        in_specs=[IN_VMEM] * 2,
        out_specs=IN_VMEM,
        scratch_shapes=[scratch(cols // LANES, LANES), scratch(rows // LANES, LANES)]
        + [scratch(LANES, LANES)] * 4,
        compiler_params=params(),
        name="row_pass",
    )(score, parts)


def in_vmem(*arrays):
    return [pltpu.with_memory_space_constraint(array, pltpu.VMEM) for array in arrays]


def col_pass_call(score, parts, count, copies):
    rows, cols = score.shape
    kept = (rows // LANES * SUB, cols)
    red_f, part, *table = pl.pallas_call(
        functools.partial(col_kernel, count),
        out_shape=(
            pltpu.VMEM((rows // LANES, LANES), jnp.float32),
            vecs(copies, cols),
            pltpu.VMEM((rows, cols), jnp.bfloat16),
            pltpu.VMEM(kept, jnp.float32),
        ),
        in_specs=[IN_VMEM] * 2,
        out_specs=(IN_VMEM,) * 4,
        scratch_shapes=[scratch(*kept)] + [scratch(LANES, LANES)] * 2,
        compiler_params=params(),
        name="col_pass",
    )(*in_vmem(score), parts)
    return red_f, part, table


def last_col_call(score, parts, table, before, count, copies):
    rows, cols = score.shape
    return pl.pallas_call(
        functools.partial(last_col_kernel, count),
        out_shape=(pltpu.VMEM((rows // LANES, LANES), jnp.float32), vecs(copies, cols)),
        in_specs=[IN_VMEM] * 5,
        out_specs=(IN_VMEM, IN_VMEM),
        scratch_shapes=[scratch(rows // LANES, LANES)]
        + [scratch(rows // LANES * SUB, cols)] * 2
        + [scratch(LANES, LANES)] * 2,
        compiler_params=params(),
        name="last_col_pass",
    )(*in_vmem(score), parts, *in_vmem(*table, before))


def last_call(parts, pot_f, src_sq, tgt_sq, count):
    return pl.pallas_call(
        functools.partial(last_kernel, count),
        out_shape=(vec(src_sq.size), vec(tgt_sq.size)),
        in_specs=[IN_VMEM] * 4,
        out_specs=(IN_VMEM, IN_VMEM),
        compiler_params=params(),
        name="last",
    )(parts, pltpu.with_memory_space_constraint(pot_f, pltpu.VMEM), src_sq, tgt_sq)


def exchange(part, axis):
    return lax.all_to_all(part, axis, 0, 0, tiled=True)


def move(block, to):
    pairs = []
    for z, core, y, x in itertools.product(range(4), range(2), range(4), range(4)):
        a, b, c, d = to(z, core, y, x)
        pairs.append((((z * 2 + core) * 4 + y) * 4 + x, ((a % 4 * 2 + b) * 4 + c % 4) * 4 + d % 4))
    return lax.ppermute(block, ("src", "tgt"), pairs)


def other_core(block):
    return move(block, lambda z, core, y, x: (z, 1 - core, y, x))


def round_z(block):
    return move(block, lambda z, core, y, x: (z + 1 - 2 * core, core, y, x))


def along_line(block, by):
    return move(block, lambda z, core, y, x: (z, core, y + core * by, x + (1 - core) * by))


def across_lines(block, by):
    return move(block, lambda z, core, y, x: (z, core, y + (1 - core) * by, x + core * by))


def after(values, earlier):
    def kernel(*refs):
        del refs

    return pl.pallas_call(
        kernel,
        out_shape=tuple(jax.ShapeDtypeStruct(v.shape, v.dtype) for v in values),
        in_specs=[ANYWHERE] * (len(values) + 1),
        out_specs=(ANYWHERE,) * len(values),
        input_output_aliases={i: i for i in range(len(values))},
        cost_estimate=pl.CostEstimate(flops=0, bytes_accessed=40_000_000, transcendentals=0),
        compiler_params=params(),
        name="after",
    )(*values, earlier)


def gather_targets(own, earlier):
    side = round_z(own)
    other = other_core(own)
    later_side, later_other = after((side, other), earlier)
    far, side_other = round_z(later_side), round_z(later_other)
    return other, side, side_other, far, other_core(side), other_core(side_other), other_core(far)


def local(src_points, tgt_points, tgt_start):
    n_src, n_tgt = lax.axis_size("src"), lax.axis_size("tgt")
    own, size = src_points, src_points.shape[0]
    total_src = size * n_tgt * n_src
    total_tgt = tgt_points.shape[0] * n_src * n_tgt
    held, tgt_held, start = bring(own, tgt_points, tgt_start.reshape(-1, LANES))

    line = jnp.concatenate([held, along_line(own, 2), along_line(own, 1), along_line(own, -1)])
    before, behind = across_lines(line, 1), across_lines(line, -1)
    far = across_lines(before, 1)

    targets, tgt_sq, red_g = place(tgt_held, *gather_targets(tgt_points, line), start)
    targets = pltpu.with_memory_space_constraint(targets, pltpu.VMEM)
    state = own_pass(line, targets, red_g, size * n_tgt)
    for points, block in ((before, 12), (behind, 4)):
        score, part, src_sq = more_pass(state, (points,), (block,), targets, red_g, 1)
        state = score, part[0], src_sq
    score, part, src_sq = more_pass(state, (far,), (8,), targets, red_g, n_tgt)
    score = pltpu.with_memory_space_constraint(score, pltpu.VMEM)
    parts = exchange(part, "tgt")
    first_f, part, table = col_pass_call(score, parts, total_tgt, n_src)
    parts = exchange(part, "src")
    part = row_pass_call(score, parts, total_src, n_tgt)
    parts = exchange(part, "tgt")
    red_f, part = last_col_call(score, parts, table, first_f, total_tgt, n_src)
    parts = exchange(part, "src")
    pot_f, pot_g = last_call(parts, red_f, src_sq, tgt_sq, total_src)
    return (pot_f.reshape(-1), pot_g.reshape(-1))


def solution(mesh):
    return jax.shard_map(
        local,
        mesh=mesh,
        in_specs=(P(("src", "tgt"), None), P(("tgt", "src"), None), P("tgt")),
        out_specs=(P("src"), P("tgt")),
        check_vma=False,
    )
```

```python
import functools
import itertools
import math

import jax
import jax.numpy as jnp
from jax import lax
from jax.experimental import pallas as pl
from jax.experimental.pallas import tpu as pltpu
from jax.sharding import PartitionSpec as P

EPSILON = 0.05
UNIT = EPSILON * math.log(2.0)

LANES = 128
SUB = 8
VMEM_LIMIT = 12 * 1024 * 1024


def tree(op, values):
    values = list(values)
    while len(values) > 1:
        values = [
            op(values[i], values[i + 1]) if i + 1 < len(values) else values[i]
            for i in range(0, len(values), 2)
        ]
    return values[0]


def merge(peaks, totals):
    peak = jnp.max(peaks, axis=0, keepdims=True)
    return peak + jnp.log2(jnp.sum(totals * jnp.exp2(peaks - peak), axis=0, keepdims=True))


def merge_parts(parts_ref, count, out_ref):
    parts = [parts_ref[i] for i in range(parts_ref.shape[0])]
    peak = tree(jnp.maximum, parts)
    total = tree(jnp.add, [jnp.exp2(part - peak) for part in parts])
    out_ref[...] = math.log2(count) - (peak + jnp.log2(total))


def repeat(part_ref, part):
    for copy in range(part_ref.shape[0]):
        part_ref[copy] = part


def power_sum(tiles, peak):
    return tree(jnp.add, [jnp.exp2(tile - peak) for tile in tiles])


def lane_tiles(rows):
    return [rows[:, k : k + LANES] for k in range(0, rows.shape[1], LANES)]


def reduce_rows(score_ref, start, groups, pots, peaks, totals):
    for group in groups:
        rows = pl.ds(start + group * SUB, SUB)
        tiles = [tile + pot for tile, pot in zip(lane_tiles(score_ref[rows, :]), pots)]
        peak = tree(jnp.maximum, tiles)
        at = group * SUB
        peaks[at : at + SUB, :] = peak
        totals[at : at + SUB, :] = power_sum(tiles, peak)


def merge_rows(peaks, totals):
    return merge(peaks[...].T, totals[...].T)


def pot_rows(pot_ref):
    return [
        jnp.broadcast_to(pot_ref[k : k + 1, :], (SUB, LANES)) for k in range(pot_ref.shape[0])
    ]


def squares(points):
    wide = points.astype(jnp.float32)
    return jnp.sum(tree(jnp.add, lane_tiles(wide * wide)).T, axis=0, keepdims=True)


def place_kernel(
    own_ref, other_ref, side_ref, side_other_ref, far_ref, theirs_ref, theirs_far_ref, start_ref, targets, sq_ref, pot_ref
):
    own = lax.axis_index("src")
    core = own % 2
    size = own_ref.shape[0]
    chips = targets.shape[0] // (2 * size)

    def put(points, chip, core):
        index = (own // 2 + chip + chips) % chips * 2 + core
        targets[pl.ds(pl.multiple_of(index * size, size), size), :] = points
        per = size // LANES
        for sub in range(per):
            row = squares(points[sub * LANES : (sub + 1) * LANES])
            sq_ref[pl.ds(index * per + sub, 1), :] = row

    side = 2 * core - 1
    put(own_ref[...], 0, core)
    put(other_ref[...], 0, 1 - core)
    put(side_ref[...], side, core)
    put(side_other_ref[...], side, 1 - core)
    put(far_ref[...], 2, core)
    put(theirs_ref[:size, :], -side, 1 - core)
    put(theirs_ref[size:, :], -side, core)
    put(theirs_far_ref[...], 2, 1 - core)
    pot_ref[...] = (start_ref[...] - sq_ref[...]) * (1.0 / UNIT)


def bring_kernel(*refs):
    count = len(refs) // 3
    copies = [
        pltpu.make_async_copy(refs[i], refs[count + i], refs[2 * count + i]) for i in range(count)
    ]
    for copy in copies:
        copy.start()
    for copy in copies:
        copy.wait()


CHUNK = 1024


def row_index(block):
    own, core = lax.axis_index("tgt"), lax.axis_index("src") % 2
    y, x = own // 4, own % 4
    line, place = y + core * (x - y), x + core * (y - x)
    at = block % 4
    by = at + (at + 3) // 4 + at // 3
    to_line, to_place = (line + block // 4) % 4, (place + by) % 4
    return to_line * (4 - 3 * core) + to_place * (1 + 3 * core)


def block_pipeline(sources, tgt_ref, pot_ref, score_ref, rows_ref, sq_ref, peaks, totals):
    per = STEP // LANES
    chunks = tgt_ref.shape[0] // CHUNK
    pots = pot_rows(pot_ref)

    def product(at, chunk):
        ref, first, block = sources[at]
        points = ref[first : first + STEP, :]
        lanes = slice(chunk * CHUNK, (chunk + 1) * CHUNK)
        score_ref[block * LANES : (block + per) * LANES, lanes] = lax.dot_general(
            points, tgt_ref[lanes, :], (((1,), (1,)), ((), ())), preferred_element_type=jnp.float32
        ) * (2.0 / UNIT)
        if chunk < per:
            row = squares(points[chunk * LANES : (chunk + 1) * LANES])
            sq_ref[pl.ds(row_index(block + chunk), 1), :] = row

    def reduce(at, chunk):
        share = chunks // per
        sub, part = chunk // share, chunk % share
        held = at % 2 * per + sub
        start = (sources[at][2] + sub) * LANES
        size = LANES // SUB // share
        groups = range(part * size, (part + 1) * size)
        reduce_rows(score_ref, start, groups, pots, peaks[held], totals[held])

    def finish(at):
        for sub in range(per):
            held = at % 2 * per + sub
            row = merge_rows(peaks[held], totals[held])
            rows_ref[pl.ds(row_index(sources[at][2] + sub), 1), :] = row

    for chunk in range(chunks):
        product(0, chunk)
    for at in range(len(sources)):
        for chunk in range(chunks):
            if at + 1 < len(sources):
                product(at + 1, chunk)
            reduce(at, chunk)
            if at and chunk == chunks // 2:
                finish(at - 1)
    finish(len(sources) - 1)


def own_kernel(points_ref, tgt_ref, pot_ref, score_ref, rows_ref, src_sq_ref, *held):
    sources = [(points_ref, 0, 0), (points_ref, STEP, 2)]
    block_pipeline(sources, tgt_ref, pot_ref, score_ref, rows_ref, src_sq_ref, held[:4], held[4:])


def more_kernel(
    blocks, score_in_ref, rows_in_ref, src_sq_in_ref, tgt_ref, pot_ref, *refs
):
    point_refs, refs = refs[: len(blocks)], refs[len(blocks) :]
    score_ref, part_ref, src_sq_ref, rows_ref, *held = refs
    rows_ref[...] = rows_in_ref[...]
    src_sq_ref[...] = src_sq_in_ref[...]
    sources = [
        (ref, first, block + first // LANES)
        for ref, block in zip(point_refs, blocks)
        for first in range(0, ref.shape[0], STEP)
    ]
    block_pipeline(sources, tgt_ref, pot_ref, score_ref, rows_ref, src_sq_ref, held[:4], held[4:])
    repeat(part_ref, rows_ref[...])


def two_by_two(blocks, step):
    step(1, False)

    @pl.loop(1, blocks // 2)
    def _(pair):
        step(2 * pair, True)
        step(2 * pair + 1, False)


def row_kernel(count, score_ref, parts_ref, part_ref, pot_ref, rows_ref, *held):
    merge_parts(parts_ref, count, pot_ref)
    pots = pot_rows(pot_ref)
    blocks = score_ref.shape[0] // LANES
    even, odd = held[:2], held[2:]

    def reduce(block, into):
        start = pl.multiple_of(block * LANES, LANES)
        reduce_rows(score_ref, start, range(LANES // SUB), pots, *into)

    def finish(block, held):
        rows_ref[pl.ds(row_index(block), 1), :] = merge_rows(*held)

    def step(block, is_even):
        finish(block - 1, odd if is_even else even)
        reduce(block, even if is_even else odd)

    reduce(0, even)
    two_by_two(blocks, step)
    finish(blocks - 1, odd)
    repeat(part_ref, rows_ref[...])


def by_row_blocks(pot_ref, blocks, reduce, even, odd):
    def widen(block, into):
        row = pot_ref[pl.ds(row_index(block), 1), :]
        into[...] = jnp.broadcast_to(row, (LANES, LANES)).T

    def run(block, wide):
        here = pl.ds(pl.multiple_of(block * LANES, LANES), LANES)
        reduce(here, pl.ds(block, 1), wide[...])

    def step(block, is_even):
        widen(block, even if is_even else odd)
        run(block - 1, odd if is_even else even)

    widen(0, even)
    two_by_two(blocks, step)
    run(blocks - 1, odd)


def column_tiles(cols):
    return [slice(k, k + LANES) for k in range(0, cols, LANES)]


def row_groups(tile):
    return [tile[i : i + SUB] for i in range(0, LANES, SUB)]


def exact_columns(score_ref, pot_ref, part_ref, peaks, totals, even, odd, table_ref=None):
    rows, cols = score_ref.shape

    def reduce(here, there, pots):
        for k, lanes in enumerate(column_tiles(cols)):
            tiles = row_groups(score_ref[here, lanes] + pots)
            peak = jnp.max(tree(jnp.maximum, tiles), axis=0, keepdims=True)
            powers = [jnp.exp2(tile - peak) for tile in tiles]
            peaks[k, there, :] = peak
            totals[k, there, :] = jnp.sum(tree(jnp.add, powers), axis=0, keepdims=True)
            if table_ref is not None:
                table_ref[here, lanes] = jnp.concatenate(powers, axis=0).astype(jnp.bfloat16)

    by_row_blocks(pot_ref, rows // LANES, reduce, even, odd)
    for k in range(cols // LANES):
        part_ref[0, k : k + 1, :] = merge(peaks[k], totals[k])


def col_kernel(
    count, score_ref, parts_ref, pot_ref, part_ref, table_ref, peaks, totals, even, odd
):
    merge_parts(parts_ref, count, pot_ref)
    exact_columns(score_ref, pot_ref, part_ref, peaks, totals, even, odd, table_ref)
    repeat(part_ref, part_ref[0])


FLOOR = 1e-28
LARGEST = 1e30


def last_col_kernel(
    count, score_ref, parts_ref, table_ref, kept_ref, before_ref, pot_ref, part_ref,
    ratio_ref, peaks, totals, even, odd,
):
    merge_parts(parts_ref, count, pot_ref)
    ratio = jnp.exp2(pot_ref[...] - before_ref[...])
    ratio_ref[...] = ratio
    rows, cols = score_ref.shape

    def reduce(here, there, weights):
        for k, lanes in enumerate(column_tiles(cols)):
            tile = table_ref[here, lanes].astype(jnp.float32) * weights
            total = tree(jnp.add, row_groups(tile))
            totals[k, there, :] = jnp.sum(total, axis=0, keepdims=True)

    by_row_blocks(ratio_ref, rows // LANES, reduce, even, odd)
    sums = []
    for k in range(cols // LANES):
        peak = jnp.max(kept_ref[k], axis=0, keepdims=True)
        scaled = totals[k] * jnp.exp2(kept_ref[k] - peak)
        sums.append(jnp.sum(scaled, axis=0, keepdims=True))
        part_ref[0, k : k + 1, :] = peak + jnp.log2(sums[-1])

    largest, least = jnp.max(ratio), jnp.min(tree(jnp.minimum, sums))
    whole = (largest <= LARGEST) & (least >= FLOOR * jnp.maximum(largest, 1.0))

    @pl.when(jnp.logical_not(whole))
    def _():
        exact_columns(score_ref, pot_ref, part_ref, peaks, totals, even, odd)

    repeat(part_ref, part_ref[0])


def last_kernel(count, parts_ref, pot_f_ref, src_sq_ref, tgt_sq_ref, out_f_ref, out_g_ref):
    out_f_ref[...] = pot_f_ref[...] * UNIT + src_sq_ref[...]
    merge_parts(parts_ref, count, out_g_ref)
    out_g_ref[...] = out_g_ref[...] * UNIT + tgt_sq_ref[...]


def params():
    return pltpu.CompilerParams(vmem_limit_bytes=VMEM_LIMIT)


def vec(size):
    return jax.ShapeDtypeStruct((size // LANES, LANES), jnp.float32)


def vecs(copies, size):
    return jax.ShapeDtypeStruct((copies, size // LANES, LANES), jnp.float32)


def scratch(*shape):
    return pltpu.VMEM(shape, jnp.float32)


ANYWHERE = pl.BlockSpec(memory_space=pl.ANY)
IN_VMEM = pl.BlockSpec(memory_space=pltpu.VMEM)


def place(own, other, side, side_other, far, theirs, theirs_far, start):
    rows, width = 8 * own.shape[0], own.shape[1]
    return pl.pallas_call(
        place_kernel,
        out_shape=(pltpu.VMEM((rows, width), own.dtype), vec(rows), vec(rows)),
        in_specs=[IN_VMEM] * 8,
        out_specs=(IN_VMEM,) * 3,
        cost_estimate=cost(rows, width, 1),
        compiler_params=params(),
        name="place",
    )(own, other, side, side_other, far, theirs, theirs_far, start)


def bring(*arrays):
    return pl.pallas_call(
        bring_kernel,
        out_shape=tuple(pltpu.VMEM(a.shape, a.dtype) for a in arrays),
        in_specs=[pl.BlockSpec(memory_space=pltpu.HBM)] * len(arrays),
        out_specs=(IN_VMEM,) * len(arrays),
        scratch_shapes=[pltpu.SemaphoreType.DMA] * len(arrays),
        compiler_params=params(),
        name="bring",
    )(*[pltpu.with_memory_space_constraint(a, pltpu.HBM) for a in arrays])


def cost(rows, cols, width):
    return pl.CostEstimate(
        flops=2 * rows * cols * width, bytes_accessed=8 * rows * cols, transcendentals=rows * cols
    )


STEP = 256


def step_scratch():
    return [scratch(LANES, LANES)] * 8


def own_pass(points, targets, pot, rows):
    cols, width = targets.shape
    return pl.pallas_call(
        own_kernel,
        out_shape=(pltpu.VMEM((rows, cols), jnp.float32), vec(rows), vec(rows)),
        in_specs=[IN_VMEM] * 3,
        out_specs=(IN_VMEM,) * 3,
        scratch_shapes=step_scratch(),
        cost_estimate=cost(points.shape[0], cols, width),
        compiler_params=params(),
        name="own_pass",
    )(points, targets, pot)


def more_pass(state, points, blocks, targets, pot, copies):
    score, row_parts, src_sq = state
    (rows, cols), width = score.shape, targets.shape[1]
    added = sum(array.shape[0] for array in points)
    score = pltpu.with_memory_space_constraint(score, pltpu.VMEM)
    return pl.pallas_call(
        functools.partial(more_kernel, blocks),
        out_shape=(pltpu.VMEM((rows, cols), jnp.float32), vecs(copies, rows), vec(rows)),
        in_specs=[IN_VMEM] * (5 + len(points)),
        out_specs=(IN_VMEM,) * 3,
        scratch_shapes=[scratch(rows // LANES, LANES)] + step_scratch(),
        input_output_aliases={0: 0},
        cost_estimate=cost(added, cols, width),
        compiler_params=params(),
        name="more_pass",
    )(score, row_parts, src_sq, targets, pot, *points)


def row_pass_call(score, parts, count, copies):
    rows, cols = score.shape
    return pl.pallas_call(
        functools.partial(row_kernel, count),
        out_shape=vecs(copies, rows),
        in_specs=[IN_VMEM] * 2,
        out_specs=IN_VMEM,
        scratch_shapes=[scratch(cols // LANES, LANES), scratch(rows // LANES, LANES)]
        + [scratch(LANES, LANES)] * 4,
        compiler_params=params(),
        name="row_pass",
    )(score, parts)


def in_vmem(*arrays):
    return [pltpu.with_memory_space_constraint(array, pltpu.VMEM) for array in arrays]


def col_pass_call(score, parts, count, copies):
    rows, cols = score.shape
    kept = (cols // LANES, rows // LANES, LANES)
    red_f, part, *table = pl.pallas_call(
        functools.partial(col_kernel, count),
        out_shape=(
            pltpu.VMEM((rows // LANES, LANES), jnp.float32),
            vecs(copies, cols),
            pltpu.VMEM((rows, cols), jnp.bfloat16),
            pltpu.VMEM(kept, jnp.float32),
        ),
        in_specs=[IN_VMEM] * 2,
        out_specs=(IN_VMEM,) * 4,
        scratch_shapes=[scratch(*kept)] + [scratch(LANES, LANES)] * 2,
        compiler_params=params(),
        name="col_pass",
    )(*in_vmem(score), parts)
    return red_f, part, table


def last_col_call(score, parts, table, before, count, copies):
    rows, cols = score.shape
    return pl.pallas_call(
        functools.partial(last_col_kernel, count),
        out_shape=(pltpu.VMEM((rows // LANES, LANES), jnp.float32), vecs(copies, cols)),
        in_specs=[IN_VMEM] * 5,
        out_specs=(IN_VMEM, IN_VMEM),
        scratch_shapes=[scratch(rows // LANES, LANES)]
        + [scratch(cols // LANES, rows // LANES, LANES)] * 2
        + [scratch(LANES, LANES)] * 2,
        compiler_params=params(),
        name="last_col_pass",
    )(*in_vmem(score), parts, *in_vmem(*table, before))


def last_call(parts, pot_f, src_sq, tgt_sq, count):
    return pl.pallas_call(
        functools.partial(last_kernel, count),
        out_shape=(vec(src_sq.size), vec(tgt_sq.size)),
        in_specs=[IN_VMEM] * 4,
        out_specs=(IN_VMEM, IN_VMEM),
        compiler_params=params(),
        name="last",
    )(parts, pltpu.with_memory_space_constraint(pot_f, pltpu.VMEM), src_sq, tgt_sq)


def exchange(part, axis):
    return lax.all_to_all(part, axis, 0, 0, tiled=True)


def move(block, to):
    pairs = []
    for z, core, y, x in itertools.product(range(4), range(2), range(4), range(4)):
        a, b, c, d = to(z, core, y, x)
        pairs.append((((z * 2 + core) * 4 + y) * 4 + x, ((a % 4 * 2 + b) * 4 + c % 4) * 4 + d % 4))
    return lax.ppermute(block, ("src", "tgt"), pairs)


def other_core(block):
    return move(block, lambda z, core, y, x: (z, 1 - core, y, x))


def round_z(block):
    return move(block, lambda z, core, y, x: (z + 1 - 2 * core, core, y, x))


def along_line(block, by):
    return move(block, lambda z, core, y, x: (z, core, y + core * by, x + (1 - core) * by))


def across_lines(block, by):
    return move(block, lambda z, core, y, x: (z, core, y + (1 - core) * by, x + core * by))


def after(value, earlier):
    def kernel(*refs):
        del refs

    return pl.pallas_call(
        kernel,
        out_shape=jax.ShapeDtypeStruct(value.shape, value.dtype),
        in_specs=[ANYWHERE] * 2,
        out_specs=ANYWHERE,
        input_output_aliases={0: 0},
        cost_estimate=pl.CostEstimate(flops=0, bytes_accessed=40_000_000, transcendentals=0),
        compiler_params=params(),
        name="after",
    )(value, earlier)


def gather_targets(own, earlier):
    side = round_z(own)
    other = other_core(own)
    far = round_z(after(side, earlier))
    side_other = round_z(other)
    theirs = other_core(jnp.concatenate([side, side_other]))
    return other, side, side_other, far, theirs, other_core(far)


def local(src_points, tgt_points, tgt_start):
    n_src, n_tgt = lax.axis_size("src"), lax.axis_size("tgt")
    own, size = src_points, src_points.shape[0]
    total_src = size * n_tgt * n_src
    total_tgt = tgt_points.shape[0] * n_src * n_tgt
    held, tgt_held, start = bring(own, tgt_points, tgt_start.reshape(-1, LANES))

    line = jnp.concatenate([held, along_line(own, 2), along_line(own, 1), along_line(own, -1)])
    before, behind = across_lines(line, 1), across_lines(line, -1)
    far = across_lines(before, 1)

    targets, tgt_sq, red_g = place(tgt_held, *gather_targets(tgt_points, line), start)
    targets = pltpu.with_memory_space_constraint(targets, pltpu.VMEM)
    state = own_pass(line, targets, red_g, size * n_tgt)
    for points, block in ((before, 12), (behind, 4)):
        score, part, src_sq = more_pass(state, (points,), (block,), targets, red_g, 1)
        state = score, part[0], src_sq
    score, part, src_sq = more_pass(state, (far,), (8,), targets, red_g, n_tgt)
    score = pltpu.with_memory_space_constraint(score, pltpu.VMEM)
    parts = exchange(part, "tgt")
    first_f, part, table = col_pass_call(score, parts, total_tgt, n_src)
    parts = exchange(part, "src")
    part = row_pass_call(score, parts, total_src, n_tgt)
    parts = exchange(part, "tgt")
    red_f, part = last_col_call(score, parts, table, first_f, total_tgt, n_src)
    parts = exchange(part, "src")
    pot_f, pot_g = last_call(parts, red_f, src_sq, tgt_sq, total_src)
    return (pot_f.reshape(-1), pot_g.reshape(-1))


def solution(mesh):
    return jax.shard_map(
        local,
        mesh=mesh,
        in_specs=(P(("src", "tgt"), None), P(("tgt", "src"), None), P("tgt")),
        out_specs=(P("src"), P("tgt")),
        check_vma=False,
    )
```
